32 devices in a mesh: row: 4 (over y, core), col: 8 (over z, x).
Axes of the slice: x: 2, y: 2, z: 4, core: 2. Of those that a mesh axis runs over, the one named last changes fastest.
Arguments:
- noise: bfloat16 [4096, 4096], P('row', 'col'), may hold values from -6 to 6
- latents: bfloat16 [8192, 4096], P('col', 'row'), may hold values from -12 to 12
Outputs:
- transported: bfloat16 [4096, 4096], P('row', 'col')
- row_potential: float32 [4096], P('row')
- col_potential: float32 [8192], P('col')
The draws below stay inside these ranges and needn't reach their ends.
All inputs are finite; a program needn't handle non-finite values.
Results may differ from the reference program's by a relative error of at most 0.018.
Values may be sent and summed in bfloat16 or wider, within the bound.
A program may use at most 64 MiB of HBM per device.

```python
import math
import jax
import jax.numpy as jnp
from jax import lax

LATDIM = 4096
COLS_DEV = 1024
ITERS = 3
NOISE = 4096
LATS = 8192
N_COL = 8


def shared_noise(key):
    values = jax.random.normal(jax.random.fold_in(key, 11), (NOISE, LATDIM), jnp.float32)
    return jnp.clip(values, -6.0, 6.0)


def draw_noise(key, part):
    base = shared_noise(key)
    values = base
    return values.astype(jnp.bfloat16)


def draw_latents(key, part):
    key = jax.random.fold_in(key, 5)
    keys = jax.random.split(key, 2)
    scale = jnp.exp(jax.random.uniform(keys[0], (LATS, 1), jnp.float32, math.log(0.4), math.log(1.6)))
    values = jax.random.normal(keys[1], (LATS, LATDIM), jnp.float32) * scale
    return jnp.clip(values, -12.0, 12.0).astype(jnp.bfloat16)


def setup_inputs(seed: int = 0) -> dict:
    key_list = jax.random.split(jax.random.key(seed), 3)
    noise = draw_noise(jax.random.fold_in(key_list[2], 71), 0)
    latents = draw_latents(jax.random.fold_in(key_list[2], 71), 0)
    return {"noise": noise, "latents": latents}


epsilon = 0.01


def logsum(scores, axis):
    high = jnp.max(scores, axis=axis, keepdims=True)
    total = jnp.sum(jnp.exp(scores - high), axis=axis)
    return jnp.squeeze(high, axis) + jnp.log(total)


def reference(noise, latents):
    cross = jnp.dot(noise, latents.T, preferred_element_type=jnp.float32)
    logits = cross * (2.0 / (LATDIM * epsilon))
    col_potential = jnp.zeros((LATS,), jnp.float32)
    row_potential = jnp.zeros((NOISE,), jnp.float32)
    for step in range(ITERS):
        row_potential = -math.log(NOISE) - logsum(logits + col_potential[None, :], 1)
        col_potential = -math.log(LATS) - logsum(logits + row_potential[:, None], 0)
    plan = jnp.exp(logits + row_potential[:, None] + col_potential[None, :]).astype(jnp.bfloat16)
    plan_blocks = jnp.transpose(plan.reshape(NOISE, N_COL, COLS_DEV), (1, 0, 2))
    lat_blocks = latents.reshape(N_COL, COLS_DEV, LATDIM)

    def add_block(total, pair):
        partial_value = jnp.dot(pair[0], pair[1], preferred_element_type=jnp.float32).astype(jnp.bfloat16)
        return total + partial_value.astype(jnp.float32), None

    numerator, unused = lax.scan(add_block, jnp.zeros((NOISE, LATDIM), jnp.float32), (plan_blocks, lat_blocks))
    mass = jnp.sum(plan.astype(jnp.float32), axis=1)
    transported = (numerator / mass[:, None]).astype(jnp.bfloat16)
    return transported, row_potential, col_potential
```

```python
import functools
import math

import jax
import jax.numpy as jnp
from jax import lax
from jax.experimental import pallas as pl
from jax.experimental.pallas import tpu as pltpu
from jax.sharding import PartitionSpec as P

ITERS = 3
EPSILON = 0.01
LANES = 128
MESH = pl.DeviceIdType.MESH


def kernel(
    nr, nc, noise, lat,
    out, row_out, col_out,
    noise_all, lat_all, logits, plan, rowb, mt, st, mc, sc, colp,
    row_box, col_box, x_send, x_recv, own, z_low, z_high, num,
    local_sem, ng_send, ng_recv, lg_send, lg_recv,
    row_send, row_recv, col_send, col_recv,
    xs_sem, xr_sem, up_sem, low_sem, down_sem, high_sem,
):
    rows, kn = noise.shape
    cols, kl = lat.shape
    width = kl * nr
    hi = nc // 2
    groups = cols // LANES
    scale = 2.0 / (width * EPSILON)
    r = lax.axis_index("row")
    c = lax.axis_index("col")
    h, l = lax.div(c, 2), lax.rem(c, 2)
    rh, rl = lax.div(r, 2), lax.rem(r, 2)

    barrier = pltpu.get_barrier_semaphore()
    for d in range(1, nc):
        pl.semaphore_signal(barrier, inc=1, device_id={"col": lax.rem(c + d, nc)}, device_id_type=MESH)
    for d in range(1, nr):
        pl.semaphore_signal(barrier, inc=1, device_id={"row": lax.rem(r + d, nr)}, device_id_type=MESH)
    pl.semaphore_wait(barrier, nc - 1 + nr - 1)

    def noise_slot(j):
        return noise_all.at[lax.div(j, 2), :, pl.ds(pl.multiple_of(lax.rem(j, 2) * kn, kn), kn)]

    def lat_slot(j):
        return lat_all.at[j]

    def remote(src, dst, send, recv, axis, target):
        return pltpu.make_async_remote_copy(
            src_ref=src, dst_ref=dst, send_sem=send, recv_sem=recv,
            device_id={axis: target}, device_id_type=MESH,
        )

    class Gather:
        def __init__(self, axis, n, own_ref, slot, send, recv, ah, al):
            self.axis, self.half, self.own, self.slot = axis, n // 2, own_ref, slot
            self.send, self.recv, self.h, self.l = send, recv, ah, al
            self.me = 2 * ah + al

        def copy(self, kind, j, src):
            target = (self.me + 1 - 2 * self.l, self.me + 2, self.me - 2)[kind]
            return remote(
                src, self.slot(j), self.send.at[kind, lax.div(j, 2)], self.recv.at[j], self.axis, target
            )

        def first(self):
            @pl.when(self.h < self.half - 1)
            def _():
                self.copy(1, self.me, self.own).start()

            @pl.when(self.h > 0)
            def _():
                self.copy(2, self.me, self.own).start()

            self.copy(0, self.me, self.own).start()

        def arrived(self, j):
            self.copy(0, j, self.slot(j)).wait_recv()

        def forward(self, s):
            @pl.when(self.h - s >= 0)
            def _():
                j = self.me - 2 * s
                self.arrived(j)

                @pl.when(self.h < self.half - 1)
                def _():
                    self.copy(1, j, self.slot(j)).start()

                self.copy(0, j, self.slot(j)).start()

            @pl.when(self.h + s < self.half)
            def _():
                j = self.me + 2 * s
                self.arrived(j)

                @pl.when(self.h > 0)
                def _():
                    self.copy(2, j, self.slot(j)).start()

                self.copy(0, j, self.slot(j)).start()

        def other(self, k):
            self.arrived(2 * k + 1 - self.l)

        def finish(self):
            @pl.loop(0, self.half)
            def _(k):
                j = 2 * k + self.l
                self.copy(0, j, self.slot(j)).wait_send()

                @pl.when((k <= self.h) & (self.h < self.half - 1))
                def _():
                    self.copy(1, j, self.slot(j)).wait_send()

                @pl.when((k >= self.h) & (self.h > 0))
                def _():
                    self.copy(2, j, self.slot(j)).wait_send()

    noise_g = Gather("col", nc, noise, noise_slot, ng_send, ng_recv, h, l)
    lat_g = Gather("row", nr, lat, lat_slot, lg_send, lg_recv, rh, rl)
    noise_g.first()
    lat_g.first()
    mine = [
        pltpu.make_async_copy(noise, noise_slot(c), local_sem.at[0]),
        pltpu.make_async_copy(lat, lat_slot(r), local_sem.at[1]),
    ]
    for copy in mine:
        copy.start()
    colp[...] = jnp.zeros_like(colp)

    tile_n = min(256, cols)

    def block(k, add):
        @pl.loop(0, cols // tile_n)
        def _(t):
            span = pl.ds(pl.multiple_of(t * tile_n, tile_n), tile_n)
            part = lax.dot_general(
                noise_all[k], lat_all[k, span, :], (((1,), (1,)), ((), ())),
                preferred_element_type=jnp.float32,
            ) * scale
            if add:
                logits[:, span] += part
            else:
                logits[:, span] = part

    def blocks(s):
        @pl.loop(0, 2)
        def _(side):
            k = h + s * (2 * side - 1)

            @pl.when((k >= 0) & (k < hi))
            def _():
                noise_g.other(k)
                block(k, True)

    for s in range(1, min(3, hi)):
        noise_g.forward(s)
    for s in range(1, nr // 2):
        lat_g.forward(s)
    for copy in mine:
        copy.wait()

    @pl.loop(0, nr // 2)
    def _(k):
        lat_g.other(k)

    noise_g.other(h)
    block(h, False)
    if hi > 1:
        blocks(1)
    for s in range(3, hi):
        noise_g.forward(s)
        blocks(s - 1)
    if hi > 2:
        blocks(hi - 1)

    def exchange(axis, n, me, box, send, recv):
        for d in range(1, n):
            remote(box.at[me], box.at[me], send.at[d], recv.at[me], axis, lax.rem(me + d, n)).start()
        for d in range(1, n):
            j = lax.rem(me + n - d, n)
            remote(box.at[j], box.at[j], send.at[d], recv.at[j], axis, j).wait_recv()

    def sent(axis, n, me, box, send, recv):
        for d in range(1, n):
            remote(box.at[me], box.at[me], send.at[d], recv.at[me], axis, lax.rem(me + d, n)).wait_send()

    def merged(n, box):
        high = functools.reduce(jnp.maximum, [box[j, 0:1, :] for j in range(n)])
        total = functools.reduce(
            jnp.add, [box[j, 1:2, :] * jnp.exp(box[j, 0:1, :] - high) for j in range(n)]
        )
        return high + jnp.log(total)

    def lane(g):
        return pl.ds(g * LANES, LANES)

    row_tile = 32
    col_tile = 64

    for step in range(ITERS):
        @pl.loop(0, rows // row_tile, unroll=2)
        def _(t):
            span = pl.ds(pl.multiple_of(t * row_tile, row_tile), row_tile)
            v = [logits[span, lane(g)] + colp[:, lane(g)] for g in range(groups)]
            m = functools.reduce(jnp.maximum, v)
            mt[span, :] = m
            st[span, :] = functools.reduce(jnp.add, [jnp.exp(x - m) for x in v])

        m = mt[...].T
        high = jnp.max(m, axis=0, keepdims=True)
        box = row_box.at[step]
        mine_box = box.at[c]
        mine_box[0:1, :] = high
        mine_box[1:2, :] = jnp.sum(st[...].T * jnp.exp(m - high), axis=0, keepdims=True)
        exchange("col", nc, c, box, row_send.at[step], row_recv.at[step])
        rowp = -math.log(rows * nr) - merged(nc, box)
        row_out[...] = rowp
        rowb[...] = jnp.broadcast_to(rowp, (LANES, rows)).T

        @pl.loop(0, rows // col_tile)
        def _(t):
            span = pl.ds(pl.multiple_of(t * col_tile, col_tile), col_tile)
            small = pl.ds(pl.multiple_of(t * 8, 8), 8)
            shift = rowb[span, :]
            for g in range(groups):
                v = (logits[span, lane(g)] + shift).reshape(col_tile // 8, 8, LANES)
                m = jnp.max(v, axis=0)
                mc[small, lane(g)] = m
                sc[small, lane(g)] = jnp.sum(jnp.exp(v - m[None]), axis=0)

        m = mc[...]
        high = jnp.max(m, axis=0, keepdims=True)
        box = col_box.at[step]
        mine_box = box.at[r]
        mine_box[0:1, :] = high
        mine_box[1:2, :] = jnp.sum(sc[...] * jnp.exp(m - high), axis=0, keepdims=True)
        exchange("row", nr, r, box, col_send.at[step], col_recv.at[step])
        colp[...] = -math.log(cols * nc) - merged(nr, box)
    col_out[...] = colp[...]

    @pl.loop(0, rows // row_tile, unroll=2)
    def _(t):
        span = pl.ds(pl.multiple_of(t * row_tile, row_tile), row_tile)
        shift = rowb[span, :]
        total = jnp.zeros((row_tile, LANES), jnp.float32)
        for g in range(groups):
            p = jnp.exp(logits[span, lane(g)] + shift + colp[:, lane(g)]).astype(jnp.bfloat16)
            plan[span, lane(g)] = p
            total += p.astype(jnp.float32)
        mt[span, :] = total

    tile_k = min(256, kn)

    def share(k, side, dst):
        @pl.loop(0, kn // tile_k)
        def _(t):
            off = pl.multiple_of(t * tile_k, tile_k)
            src = pl.multiple_of(side * kn + t * tile_k, tile_k)
            dst[:, pl.ds(off, tile_k)] = jnp.dot(
                plan[...], lat_all[k, :, pl.ds(src, tile_k)], preferred_element_type=jnp.float32
            ).astype(jnp.bfloat16)

    partner = c + 1 - 2 * l

    def x_copy(k):
        return remote(x_send.at[k], x_recv.at[k], xs_sem.at[k], xr_sem.at[k], "col", partner)

    def up_copy(k):
        return remote(own.at[k], z_low.at[k], up_sem.at[k], low_sem.at[k], "col", c + 2)

    def down_copy(k):
        return remote(own.at[k], z_high.at[k], down_sem.at[k], high_sem.at[k], "col", c - 2)

    def farthest_first(body):
        @pl.loop(0, 2 * hi - 1)
        def _(p):
            s = hi - 1 - lax.div(p, 2)
            k = h + s * (1 - 2 * lax.rem(p, 2))

            @pl.when((k >= 0) & (k < hi))
            def _():
                body(k)

    def send_share(k):
        share(k, 1 - l, x_send.at[k])
        x_copy(k).start()

    farthest_first(send_share)

    mine_box = row_box.at[ITERS, c]
    mine_box[0:1, :] = jnp.sum(mt[...].T, axis=0, keepdims=True)
    mine_box[1:2, :] = jnp.zeros((1, rows), jnp.float32)
    exchange("col", nc, c, row_box.at[ITERS], row_send.at[ITERS], row_recv.at[ITERS])
    mass = functools.reduce(jnp.add, [row_box[ITERS, j, 0:1, :] for j in range(nc)])
    rowb[...] = jnp.broadcast_to(1.0 / mass, (LANES, rows)).T

    farthest_first(lambda k: share(k, l, own.at[k]))

    f32 = jnp.float32
    add_tile = min(128, rows)

    def tiles(body):
        @pl.loop(0, rows // add_tile)
        def _(t):
            body(pl.ds(pl.multiple_of(t * add_tile, add_tile), add_tile))

    def add_two(k):
        def body(span):
            own[k, span, :] = (own[k, span, :].astype(f32) + x_recv[k, span, :].astype(f32)).astype(jnp.bfloat16)
        tiles(body)

    def add_three(k, third):
        def body(span):
            own[k, span, :] = (
                own[k, span, :].astype(f32) + x_recv[k, span, :].astype(f32) + third[k, span, :].astype(f32)
            ).astype(jnp.bfloat16)
        tiles(body)

    def relay(k):
        x_copy(k).wait_recv()

        @pl.when(k > h)
        def _():
            @pl.when(h > 0)
            def _():
                up_copy(k).wait_recv()
                add_three(k, z_low)

            @pl.when(h == 0)
            def _():
                add_two(k)

            up_copy(k).start()

        @pl.when(k < h)
        def _():
            @pl.when(h < hi - 1)
            def _():
                down_copy(k).wait_recv()
                add_three(k, z_high)

            @pl.when(h == hi - 1)
            def _():
                add_two(k)

            down_copy(k).start()

    farthest_first(relay)

    def start_sum(span):
        num[span, :] = own[h, span, :].astype(f32) + x_recv[h, span, :].astype(f32)

    tiles(start_sum)

    @pl.when(h > 0)
    def _():
        up_copy(h).wait_recv()

        def body(span):
            num[span, :] += z_low[h, span, :].astype(f32)
        tiles(body)

    @pl.when(h < hi - 1)
    def _():
        down_copy(h).wait_recv()

        def body(span):
            num[span, :] += z_high[h, span, :].astype(f32)
        tiles(body)

    def last(span):
        inverse = rowb[span, :]
        for g in range(kn // LANES):
            out[span, lane(g)] = (num[span, lane(g)] * inverse).astype(jnp.bfloat16)

    tiles(last)

    noise_g.finish()
    lat_g.finish()
    for step in range(ITERS + 1):
        sent("col", nc, c, row_box.at[step], row_send.at[step], row_recv.at[step])
    for step in range(ITERS):
        sent("row", nr, r, col_box.at[step], col_send.at[step], col_recv.at[step])

    @pl.loop(0, hi)
    def _(k):
        x_copy(k).wait_send()

        @pl.when(k > h)
        def _():
            up_copy(k).wait_send()

        @pl.when(k < h)
        def _():
            down_copy(k).wait_send()


def on_device(nr, nc, noise, latents):
    rows, kn = noise.shape
    cols, kl = latents.shape
    hi = nc // 2
    bf16, f32 = jnp.bfloat16, jnp.float32
    vmem, dma = pltpu.VMEM, pltpu.SemaphoreType.DMA
    transported, row_potential, col_potential = pl.pallas_call(
        functools.partial(kernel, nr, nc),
        out_shape=(
            jax.ShapeDtypeStruct((rows, kn), bf16),
            jax.ShapeDtypeStruct((1, rows), f32),
            jax.ShapeDtypeStruct((1, cols), f32),
        ),
        in_specs=[pl.BlockSpec(memory_space=pl.ANY)] * 2,
        out_specs=[pl.BlockSpec(memory_space=pltpu.VMEM)] * 3,
        scratch_shapes=[
            vmem((hi, rows, 2 * kn), bf16),
            vmem((nr, cols, kl), bf16),
            vmem((rows, cols), f32),
            vmem((rows, cols), bf16),
            vmem((rows, LANES), f32),
            vmem((rows, LANES), f32),
            vmem((rows, LANES), f32),
            vmem((rows // 8, cols), f32),
            vmem((rows // 8, cols), f32),
            vmem((1, cols), f32),
            vmem((ITERS + 1, nc, 2, rows), f32),
            vmem((ITERS, nr, 2, cols), f32),
            vmem((hi, rows, kn), bf16),
            vmem((hi, rows, kn), bf16),
            vmem((hi, rows, kn), bf16),
            vmem((hi, rows, kn), bf16),
            vmem((hi, rows, kn), bf16),
            vmem((rows, kn), f32),
            dma((2,)),
            dma((3, hi)), dma((nc,)),
            dma((3, nr // 2)), dma((nr,)),
            dma((ITERS + 1, nc)), dma((ITERS + 1, nc)),
            dma((ITERS, nr)), dma((ITERS, nr)),
            dma((hi,)), dma((hi,)), dma((hi,)), dma((hi,)), dma((hi,)), dma((hi,)),
        ],
        compiler_params=pltpu.CompilerParams(
            collective_id=0, has_side_effects=True, vmem_limit_bytes=58 * 2**20
        ),
        cost_estimate=pl.CostEstimate(
            flops=4 * rows * cols * kl * nr, bytes_accessed=8 * 2**20, transcendentals=7 * rows * cols
        ),
    )(noise, latents)
    return transported, row_potential.reshape(rows), col_potential.reshape(cols)


def solution(mesh):
    in_specs = (P("row", "col"), P("col", "row"))
    out_specs = (P("row", "col"), P("row"), P("col"))
    return jax.shard_map(
        functools.partial(on_device, mesh.shape["row"], mesh.shape["col"]),
        mesh=mesh, in_specs=in_specs, out_specs=out_specs, check_vma=False,
    )
```

```python
import functools
import math

import jax
import jax.numpy as jnp
from jax import lax
from jax.experimental import pallas as pl
from jax.experimental.pallas import tpu as pltpu
from jax.sharding import PartitionSpec as P

ITERS = 3
EPSILON = 0.01
LANES = 128
MESH = pl.DeviceIdType.MESH


def kernel(
    nr, nc, noise, lat,
    out, row_out, col_out,
    noise_all, lat_all, logits, plan, rowb, mt, st, mc, sc, colp,
    row_box, col_box, x_send, x_recv, own, z_low, z_high, num, turned, result, out_box, row_swap, col_swap,
    local_sem, ng_send, ng_recv, lg_send, lg_recv,
    row_send, row_recv, col_send, col_recv,
    xs_sem, xr_sem, up_sem, low_sem, down_sem, high_sem, swap_send, swap_recv, out_send, out_recv,
):
    rows, kn = noise.shape
    cols, kl = lat.shape
    width = kl * nr
    hi = nc // 2
    groups = cols // LANES
    scale = 2.0 / (width * EPSILON)
    row = lax.axis_index("row")
    col = lax.axis_index("col")
    ch, cl = lax.div(col, 2), lax.rem(col, 2)
    rh, rl = lax.div(row, 2), lax.rem(row, 2)
    r, c = 2 * rh + cl, 2 * ch + rl
    h, l = ch, rl
    turn = rl != cl
    half_r = nr // 2

    def along_col(j):
        return {"row": 2 * rh + lax.rem(j, 2), "col": 2 * lax.div(j, 2) + cl}

    def along_row(j):
        return {"row": 2 * lax.div(j, 2) + rl, "col": 2 * ch + lax.rem(j, 2)}

    across = {"row": 2 * rh + 1 - rl, "col": 2 * ch + 1 - cl}

    barrier = pltpu.get_barrier_semaphore()

    def greet(device):
        pl.semaphore_signal(barrier, inc=1, device_id=device, device_id_type=MESH)

    for d in range(1, nc):
        greet(along_col(lax.rem(c + d, nc)))
    for d in range(1, nr):
        greet(along_row(lax.rem(r + d, nr)))
    for d in range(1, half_r):
        greet({"row": 2 * lax.rem(rh + d, half_r) + 1 - rl, "col": col})
    greet(across)
    pl.semaphore_wait(barrier, nc - 1 + nr - 1 + half_r - 1 + 1)

    def noise_slot(j):
        return noise_all.at[lax.div(j, 2), :, pl.ds(pl.multiple_of(lax.rem(j, 2) * kn, kn), kn)]

    def remote(src, dst, send, recv, device):
        return pltpu.make_async_remote_copy(
            src_ref=src, dst_ref=dst, send_sem=send, recv_sem=recv,
            device_id=device, device_id_type=MESH,
        )

    class Gather:
        def __init__(self, along, n, own_ref, slot, send, recv, ah, al):
            self.along, self.half, self.own, self.slot = along, n // 2, own_ref, slot
            self.send, self.recv, self.h, self.l = send, recv, ah, al
            self.me = 2 * ah + al

        def copy(self, kind, j, src):
            target = (self.me + 1 - 2 * self.l, self.me + 2, self.me - 2)[kind]
            return remote(
                src, self.slot(j), self.send.at[kind, lax.div(j, 2)], self.recv.at[j], self.along(target)
            )

        def first(self):
            @pl.when(self.h < self.half - 1)
            def _():
                self.copy(1, self.me, self.own).start()

            @pl.when(self.h > 0)
            def _():
                self.copy(2, self.me, self.own).start()

            self.copy(0, self.me, self.own).start()

        def arrived(self, j):
            self.copy(0, j, self.slot(j)).wait_recv()

        def forward(self, s):
            @pl.when(self.h - s >= 0)
            def _():
                j = self.me - 2 * s
                self.arrived(j)

                @pl.when(self.h < self.half - 1)
                def _():
                    self.copy(1, j, self.slot(j)).start()

                self.copy(0, j, self.slot(j)).start()

            @pl.when(self.h + s < self.half)
            def _():
                j = self.me + 2 * s
                self.arrived(j)

                @pl.when(self.h > 0)
                def _():
                    self.copy(2, j, self.slot(j)).start()

                self.copy(0, j, self.slot(j)).start()

        def other(self, k):
            self.arrived(2 * k + 1 - self.l)

        def finish(self):
            @pl.loop(0, self.half)
            def _(k):
                j = 2 * k + self.l
                self.copy(0, j, self.slot(j)).wait_send()

                @pl.when((k <= self.h) & (self.h < self.half - 1))
                def _():
                    self.copy(1, j, self.slot(j)).wait_send()

                @pl.when((k >= self.h) & (self.h > 0))
                def _():
                    self.copy(2, j, self.slot(j)).wait_send()

    noise_g = Gather(along_col, nc, noise, noise_slot, ng_send, ng_recv, h, l)
    half = cols // 2

    def lat_part(j, p):
        return lat_all.at[j, pl.ds(p * half, half)]

    def lat_own(p):
        return lat.at[pl.ds(p * half, half)]

    def lat_copy(kind, j, p, src=None):
        home = {"row": 2 * rh + cl, "col": col}
        side = {"row": 2 * rh + cl, "col": 2 * ch + 1 - cl}
        up = {"row": 2 * (rh + 1) + cl, "col": col}
        down = {"row": 2 * (rh - 1) + cl, "col": col}
        device = (home, side, up, down)[kind]
        return remote(
            lat_part(j, p) if src is None else src, lat_part(j, p),
            lg_send.at[kind, j, p], lg_recv.at[j, p], device,
        )

    def lat_relay(kind, j, p):
        device = (
            None, {"row": row, "col": 2 * ch + 1 - cl},
            {"row": row + 2, "col": col}, {"row": row - 2, "col": col},
        )[kind]
        return remote(lat_part(j, p), lat_part(j, p), lg_send.at[kind, j, p], lg_recv.at[j, p], device)

    def lat_arrived(j, p):
        lat_relay(1, j, p).wait_recv()

    def lat_ends(act):
        for p in (1, 0):
            act(lat_copy(1, row, p, lat_own(p)))

            @pl.when(turn)
            def _():
                act(lat_copy(0, row, p, lat_own(p)))

        for p in (0, 1):
            @pl.when(rh < half_r - 1)
            def _():
                act(lat_copy(2, row, p, lat_own(p)))

            @pl.when(rh > 0)
            def _():
                act(lat_copy(3, row, p, lat_own(p)))

    def lat_pass(act, wait):
        @pl.when(turn)
        def _():
            for q in range(2):
                j = 2 * rh + q
                wait(j, 1)

                @pl.when(rh < half_r - 1)
                def _():
                    act(lat_relay(2, j, 1))

                @pl.when(rh > 0)
                def _():
                    act(lat_relay(3, j, 1))

        for s in range(1, half_r):
            for sign, kind in ((-1, 2), (1, 3)):
                k = rh + sign * s
                onward = (rh < half_r - 1) if sign < 0 else (rh > 0)
                valid = (k >= 0) if sign < 0 else (k < half_r)

                @pl.when(valid)
                def _():
                    for q in range(2):
                        j = 2 * k + q
                        if half_r > 2:
                            @pl.when(turn)
                            def _():
                                wait(j, 1)

                                @pl.when(onward)
                                def _():
                                    act(lat_relay(kind, j, 1))

                        @pl.when(jnp.logical_not(turn))
                        def _():
                            wait(j, 0)
                            act(lat_relay(1, j, 0))

                            @pl.when(onward)
                            def _():
                                act(lat_relay(kind, j, 0))
                                wait(j, 1)
                                act(lat_relay(kind, j, 1))

    def lat_ready(k):
        kh, kq = lax.div(k, 2), lax.rem(k, 2)
        near = kh == rh
        onward = ((kh < rh) & (rh < half_r - 1)) | ((kh > rh) & (rh > 0))

        @pl.when(turn)
        def _():
            lat_arrived(k, 0)
            if half_r == 2:
                @pl.when(jnp.logical_not(near))
                def _():
                    lat_arrived(k, 1)

        @pl.when(jnp.logical_not(turn) & near & (kq != rl))
        def _():
            lat_arrived(k, 0)
            lat_arrived(k, 1)

        @pl.when(jnp.logical_not(turn) & jnp.logical_not(near) & jnp.logical_not(onward))
        def _():
            lat_arrived(k, 1)

    noise_swap = remote(noise, turned, swap_send.at[0], swap_recv.at[0], across)

    @pl.when(turn)
    def _():
        noise_swap.start()

    @pl.when(jnp.logical_not(turn))
    def _():
        noise_g.first()

    lat_ends(lambda copy: copy.start())
    keep_noise = pltpu.make_async_copy(noise, noise_slot(c), local_sem.at[0])
    keep_turned = pltpu.make_async_copy(turned, noise_slot(c), local_sem.at[0])
    keep_lat = pltpu.make_async_copy(lat, lat_all.at[row], local_sem.at[1])

    @pl.when(jnp.logical_not(turn))
    def _():
        keep_noise.start()
        keep_lat.start()

    @pl.when(turn)
    def _():
        noise_swap.wait_recv()
        noise_g.own = turned
        noise_g.first()
        keep_turned.start()

    colp[...] = jnp.zeros_like(colp)

    tile_n = min(256, cols)

    def block(k, add):
        @pl.loop(0, cols // tile_n)
        def _(t):
            span = pl.ds(pl.multiple_of(t * tile_n, tile_n), tile_n)
            part = lax.dot_general(
                noise_all[k], lat_all[k, span, :], (((1,), (1,)), ((), ())),
                preferred_element_type=jnp.float32,
            ) * scale
            if add:
                logits[:, span] += part
            else:
                logits[:, span] = part

    def noise_ready(k):
        noise_g.other(k)

    noise_g.forward(1)
    lat_pass(lambda copy: copy.start(), lat_arrived)
    for s in range(2, hi - 1):
        noise_g.forward(s)

    @pl.when(jnp.logical_not(turn))
    def _():
        keep_noise.wait()
        keep_lat.wait()

    @pl.when(turn)
    def _():
        keep_turned.wait()

    near = jnp.minimum(jnp.maximum(h, 2 * rh), 2 * rh + 1)
    noise_ready(near)
    lat_ready(near)
    block(near, False)
    if hi > 2:
        noise_g.forward(hi - 1)

    @pl.loop(1, hi)
    def _(i):
        k = jnp.where(i == 1, 4 * rh + 1 - near, lax.rem(2 * rh + i, hi))
        noise_ready(k)
        lat_ready(k)
        block(k, True)

    def exchange(along, n, me, box, send, recv):
        for d in range(1, n):
            remote(box.at[me], box.at[me], send.at[d], recv.at[me], along(lax.rem(me + d, n))).start()
        for d in range(1, n):
            j = lax.rem(me + n - d, n)
            remote(box.at[j], box.at[j], send.at[d], recv.at[j], along(j)).wait_recv()

    def sent(along, n, me, box, send, recv):
        for d in range(1, n):
            remote(box.at[me], box.at[me], send.at[d], recv.at[me], along(lax.rem(me + d, n))).wait_send()

    def merged(n, box):
        high = functools.reduce(jnp.maximum, [box[j, 0:1, :] for j in range(n)])
        total = functools.reduce(
            jnp.add, [box[j, 1:2, :] * jnp.exp(box[j, 0:1, :] - high) for j in range(n)]
        )
        return high + jnp.log(total)

    def lane(g):
        return pl.ds(g * LANES, LANES)

    row_tile = 32
    col_tile = 64

    for step in range(ITERS):
        @pl.loop(0, rows // row_tile, unroll=2)
        def _(t):
            span = pl.ds(pl.multiple_of(t * row_tile, row_tile), row_tile)
            v = [logits[span, lane(g)] + colp[:, lane(g)] for g in range(groups)]
            m = functools.reduce(jnp.maximum, v)
            mt[span, :] = m
            st[span, :] = functools.reduce(jnp.add, [jnp.exp(x - m) for x in v])

        m = mt[...].T
        high = jnp.max(m, axis=0, keepdims=True)
        box = row_box.at[step]
        mine_box = box.at[c]
        mine_box[0:1, :] = high
        mine_box[1:2, :] = jnp.sum(st[...].T * jnp.exp(m - high), axis=0, keepdims=True)
        exchange(along_col, nc, c, box, row_send.at[step], row_recv.at[step])
        rowp = -math.log(rows * nr) - merged(nc, box)
        row_swap[0] = rowp
        rowb[...] = jnp.broadcast_to(rowp, (LANES, rows)).T

        @pl.loop(0, rows // col_tile)
        def _(t):
            span = pl.ds(pl.multiple_of(t * col_tile, col_tile), col_tile)
            small = pl.ds(pl.multiple_of(t * 8, 8), 8)
            shift = rowb[span, :]
            for g in range(groups):
                v = (logits[span, lane(g)] + shift).reshape(col_tile // 8, 8, LANES)
                m = jnp.max(v, axis=0)
                mc[small, lane(g)] = m
                sc[small, lane(g)] = jnp.sum(jnp.exp(v - m[None]), axis=0)

        m = mc[...]
        high = jnp.max(m, axis=0, keepdims=True)
        box = col_box.at[step]
        mine_box = box.at[r]
        mine_box[0:1, :] = high
        mine_box[1:2, :] = jnp.sum(sc[...] * jnp.exp(m - high), axis=0, keepdims=True)
        exchange(along_row, nr, r, box, col_send.at[step], col_recv.at[step])
        colp[...] = -math.log(cols * nc) - merged(nr, box)
    row_pair = remote(row_swap.at[0], row_swap.at[1], swap_send.at[1], swap_recv.at[1], across)
    col_pair = remote(colp, col_swap, swap_send.at[2], swap_recv.at[2], across)

    @pl.when(turn)
    def _():
        row_pair.start()
        col_pair.start()

    @pl.when(jnp.logical_not(turn))
    def _():
        row_out[...] = row_swap[0]
        col_out[...] = colp[...]


    @pl.loop(0, rows // row_tile, unroll=2)
    def _(t):
        span = pl.ds(pl.multiple_of(t * row_tile, row_tile), row_tile)
        shift = rowb[span, :]
        total = jnp.zeros((row_tile, LANES), jnp.float32)
        for g in range(groups):
            p = jnp.exp(logits[span, lane(g)] + shift + colp[:, lane(g)]).astype(jnp.bfloat16)
            plan[span, lane(g)] = p
            total += p.astype(jnp.float32)
        mt[span, :] = total

    tile_k = min(256, kn)

    def share(k, side, dst):
        @pl.loop(0, kn // tile_k)
        def _(t):
            off = pl.multiple_of(t * tile_k, tile_k)
            src = pl.multiple_of(side * kn + t * tile_k, tile_k)
            dst[:, pl.ds(off, tile_k)] = jnp.dot(
                plan[...], lat_all[k, :, pl.ds(src, tile_k)], preferred_element_type=jnp.float32
            ).astype(jnp.bfloat16)

    parts = 2
    part = rows // parts
    add_tile = min(128, part)

    def piece(ref, k, p):
        return ref.at[k, pl.ds(p * part, part)]

    def x_copy(k):
        return remote(x_send.at[k], x_recv.at[k], xs_sem.at[k], xr_sem.at[k], along_col(c + 1 - 2 * l))

    def up_copy(k, p):
        return remote(
            piece(own, k, p), piece(z_low, k, p), up_sem.at[k, p], low_sem.at[k, p], along_col(c + 2)
        )

    def down_copy(k, p):
        return remote(
            piece(own, k, p), piece(z_high, k, p), down_sem.at[k, p], high_sem.at[k, p], along_col(c - 2)
        )

    def farthest_first(body):
        @pl.loop(0, 2 * hi - 1)
        def _(p):
            s = hi - 1 - lax.div(p, 2)
            k = h + s * (1 - 2 * lax.rem(p, 2))

            @pl.when((k >= 0) & (k < hi))
            def _():
                body(k)

    def send_share(k):
        share(k, 1 - l, x_send.at[k])
        x_copy(k).start()

    f32, bf16 = jnp.float32, jnp.bfloat16

    def tiles(p, body):
        @pl.loop(0, part // add_tile)
        def _(t):
            body(pl.ds(pl.multiple_of(p * part + t * add_tile, add_tile), add_tile))

    def add(k, p, third):
        def body(span):
            total = own[k, span, :].astype(f32) + third[k, span, :].astype(f32)
            own[k, span, :] = total.astype(bf16)
        tiles(p, body)

    def first_relay(k):
        x_copy(k).wait_recv()
        for p in range(parts):
            add(k, p, x_recv)

            @pl.when((k > h) & (h == 0))
            def _():
                up_copy(k, p).start()

            @pl.when((k < h) & (h == hi - 1))
            def _():
                down_copy(k, p).start()

    def work(k):
        send_share(k)
        share(k, l, own.at[k])
        first_relay(k)

    farthest_first(work)

    mine_box = row_box.at[ITERS, c]
    mine_box[0:1, :] = jnp.sum(mt[...].T, axis=0, keepdims=True)
    mine_box[1:2, :] = jnp.zeros((1, rows), f32)
    exchange(along_col, nc, c, row_box.at[ITERS], row_send.at[ITERS], row_recv.at[ITERS])
    mass = functools.reduce(jnp.add, [row_box[ITERS, j, 0:1, :] for j in range(nc)])
    rowb[...] = jnp.broadcast_to(1.0 / mass, (LANES, rows)).T

    def relay(k):
        for p in range(parts):
            @pl.when((k > h) & (h > 0))
            def _():
                up_copy(k, p).wait_recv()
                add(k, p, z_low)
                up_copy(k, p).start()

            @pl.when((k < h) & (h < hi - 1))
            def _():
                down_copy(k, p).wait_recv()
                add(k, p, z_high)
                down_copy(k, p).start()

    farthest_first(relay)

    def out_copy(p):
        span = pl.ds(p * part, part)
        return remote(result.at[span], out_box.at[span], out_send.at[p], out_recv.at[p], across)

    for p in range(parts):
        def start_sum(span):
            num[span, :] = own[h, span, :].astype(f32)

        tiles(p, start_sum)

        def add_low(span):
            num[span, :] += z_low[h, span, :].astype(f32)

        def add_high(span):
            num[span, :] += z_high[h, span, :].astype(f32)

        @pl.when(h > 0)
        def _():
            up_copy(h, p).wait_recv()
            tiles(p, add_low)

        @pl.when(h < hi - 1)
        def _():
            down_copy(h, p).wait_recv()
            tiles(p, add_high)

        def divide(ref):
            def body(span):
                inverse = rowb[span, :]
                for g in range(kn // LANES):
                    ref[span, lane(g)] = (num[span, lane(g)] * inverse).astype(bf16)
            tiles(p, body)

        @pl.when(turn)
        def _():
            divide(result)
            out_copy(p).start()

        @pl.when(jnp.logical_not(turn))
        def _():
            divide(out)

    @pl.when(turn)
    def _():
        row_pair.wait()
        col_pair.wait()
        row_out[...] = row_swap[1]
        col_out[...] = col_swap[...]
        for p in range(parts):
            out_copy(p).wait_recv()

            def body(span):
                out[span, :] = out_box[span, :]
            tiles(p, body)
        for p in range(parts):
            out_copy(p).wait_send()
        noise_swap.wait_send()

    noise_g.finish()
    lat_ends(lambda copy: copy.wait_send())
    lat_pass(lambda copy: copy.wait_send(), lambda j, p: None)
    for step in range(ITERS + 1):
        sent(along_col, nc, c, row_box.at[step], row_send.at[step], row_recv.at[step])
    for step in range(ITERS):
        sent(along_row, nr, r, col_box.at[step], col_send.at[step], col_recv.at[step])

    @pl.loop(0, hi)
    def _(k):
        x_copy(k).wait_send()

        for p in range(parts):
            @pl.when(k > h)
            def _():
                up_copy(k, p).wait_send()

            @pl.when(k < h)
            def _():
                down_copy(k, p).wait_send()


def on_device(nr, nc, noise, latents):
    rows, kn = noise.shape
    cols, kl = latents.shape
    hi = nc // 2
    bf16, f32 = jnp.bfloat16, jnp.float32
    vmem, dma = pltpu.VMEM, pltpu.SemaphoreType.DMA
    transported, row_potential, col_potential = pl.pallas_call(
        functools.partial(kernel, nr, nc),
        out_shape=(
            jax.ShapeDtypeStruct((rows, kn), bf16),
            jax.ShapeDtypeStruct((1, rows), f32),
            jax.ShapeDtypeStruct((1, cols), f32),
        ),
        in_specs=[pl.BlockSpec(memory_space=pl.ANY)] * 2,
        out_specs=[pl.BlockSpec(memory_space=pltpu.VMEM)] * 3,
        scratch_shapes=[
            vmem((hi, rows, 2 * kn), bf16),
            vmem((nr, cols, kl), bf16),
            vmem((rows, cols), f32),
            vmem((rows, cols), bf16),
            vmem((rows, LANES), f32),
            vmem((rows, LANES), f32),
            vmem((rows, LANES), f32),
            vmem((rows // 8, cols), f32),
            vmem((rows // 8, cols), f32),
            vmem((1, cols), f32),
            vmem((ITERS + 1, nc, 2, rows), f32),
            vmem((ITERS, nr, 2, cols), f32),
            vmem((hi, rows, kn), bf16),
            vmem((hi, rows, kn), bf16),
            vmem((hi, rows, kn), bf16),
            vmem((hi, rows, kn), bf16),
            vmem((hi, rows, kn), bf16),
            vmem((rows, kn), f32),
            vmem((rows, kn), bf16),
            vmem((rows, kn), bf16),
            vmem((rows, kn), bf16),
            vmem((2, 1, rows), f32),
            vmem((1, cols), f32),
            dma((2,)),
            dma((3, hi)), dma((nc,)),
            dma((4, nr, 2)), dma((nr, 2)),
            dma((ITERS + 1, nc)), dma((ITERS + 1, nc)),
            dma((ITERS, nr)), dma((ITERS, nr)),
            dma((hi,)), dma((hi,)), dma((hi, 2)), dma((hi, 2)), dma((hi, 2)), dma((hi, 2)),
            dma((3,)), dma((3,)), dma((2,)), dma((2,)),
        ],
        compiler_params=pltpu.CompilerParams(
            collective_id=0, has_side_effects=True, vmem_limit_bytes=58 * 2**20
        ),
        cost_estimate=pl.CostEstimate(
            flops=4 * rows * cols * kl * nr, bytes_accessed=8 * 2**20, transcendentals=7 * rows * cols
        ),
    )(noise, latents)
    return transported, row_potential.reshape(rows), col_potential.reshape(cols)


def solution(mesh):
    in_specs = (P("row", "col"), P("col", "row"))
    out_specs = (P("row", "col"), P("row"), P("col"))
    return jax.shard_map(
        functools.partial(on_device, mesh.shape["row"], mesh.shape["col"]),
        mesh=mesh, in_specs=in_specs, out_specs=out_specs, check_vma=False,
    )
```

```python
import functools
import math

import jax
import jax.numpy as jnp
from jax import lax
from jax.experimental import pallas as pl
from jax.experimental.pallas import tpu as pltpu
from jax.sharding import PartitionSpec as P

ITERS = 3
EPSILON = 0.01
LANES = 128
MESH = pl.DeviceIdType.MESH


def kernel(
    nr, nc, noise, lat,
    out, row_out, col_out,
    noise_all, lat_all, logits, plan, rowb, mt, st, mc, sc, colp,
    row_box, col_box, x_send, x_recv, own, z_low, z_high, num, turned, result, out_box, row_swap, col_swap,
    local_sem, ng_send, ng_recv, lg_send, lg_recv,
    row_send, row_recv, col_send, col_recv,
    xs_sem, xr_sem, up_sem, low_sem, down_sem, high_sem, swap_send, swap_recv, out_send, out_recv,
):
    rows, kn = noise.shape
    cols, kl = lat.shape
    width = kl * nr
    hi = nc // 2
    groups = cols // LANES
    scale = 2.0 / (width * EPSILON)
    row = lax.axis_index("row")
    col = lax.axis_index("col")
    ch, cl = lax.div(col, 2), lax.rem(col, 2)
    rh, rl = lax.div(row, 2), lax.rem(row, 2)
    r, c = 2 * rh + cl, 2 * ch + rl
    h, l = ch, rl
    turn = rl != cl
    half_r = nr // 2

    def along_col(j):
        return {"row": 2 * rh + lax.rem(j, 2), "col": 2 * lax.div(j, 2) + cl}

    def along_row(j):
        return {"row": 2 * lax.div(j, 2) + rl, "col": 2 * ch + lax.rem(j, 2)}

    across = {"row": 2 * rh + 1 - rl, "col": 2 * ch + 1 - cl}

    barrier = pltpu.get_barrier_semaphore()

    def greet(device):
        pl.semaphore_signal(barrier, inc=1, device_id=device, device_id_type=MESH)

    for d in range(1, nc):
        greet(along_col(lax.rem(c + d, nc)))
    for d in range(1, nr):
        greet(along_row(lax.rem(r + d, nr)))
    for d in range(1, half_r):
        greet({"row": 2 * lax.rem(rh + d, half_r) + 1 - rl, "col": col})
    greet(across)
    pl.semaphore_wait(barrier, nc - 1 + nr - 1 + half_r - 1 + 1)

    def noise_slot(j):
        return noise_all.at[lax.div(j, 2), :, pl.ds(pl.multiple_of(lax.rem(j, 2) * kn, kn), kn)]

    def remote(src, dst, send, recv, device):
        return pltpu.make_async_remote_copy(
            src_ref=src, dst_ref=dst, send_sem=send, recv_sem=recv,
            device_id=device, device_id_type=MESH,
        )

    class Gather:
        def __init__(self, along, n, own_ref, slot, send, recv, ah, al):
            self.along, self.half, self.own, self.slot = along, n // 2, own_ref, slot
            self.send, self.recv, self.h, self.l = send, recv, ah, al
            self.me = 2 * ah + al

        def copy(self, kind, j, src):
            target = (self.me + 1 - 2 * self.l, self.me + 2, self.me - 2)[kind]
            return remote(
                src, self.slot(j), self.send.at[kind, lax.div(j, 2)], self.recv.at[j], self.along(target)
            )

        def first(self):
            @pl.when(self.h < self.half - 1)
            def _():
                self.copy(1, self.me, self.own).start()

            @pl.when(self.h > 0)
            def _():
                self.copy(2, self.me, self.own).start()

            self.copy(0, self.me, self.own).start()

        def arrived(self, j):
            self.copy(0, j, self.slot(j)).wait_recv()

        def forward(self, s):
            @pl.when(self.h - s >= 0)
            def _():
                j = self.me - 2 * s
                self.arrived(j)

                @pl.when(self.h < self.half - 1)
                def _():
                    self.copy(1, j, self.slot(j)).start()

                self.copy(0, j, self.slot(j)).start()

            @pl.when(self.h + s < self.half)
            def _():
                j = self.me + 2 * s
                self.arrived(j)

                @pl.when(self.h > 0)
                def _():
                    self.copy(2, j, self.slot(j)).start()

                self.copy(0, j, self.slot(j)).start()

        def other(self, k):
            self.arrived(2 * k + 1 - self.l)

        def finish(self):
            @pl.loop(0, self.half)
            def _(k):
                j = 2 * k + self.l
                self.copy(0, j, self.slot(j)).wait_send()

                @pl.when((k <= self.h) & (self.h < self.half - 1))
                def _():
                    self.copy(1, j, self.slot(j)).wait_send()

                @pl.when((k >= self.h) & (self.h > 0))
                def _():
                    self.copy(2, j, self.slot(j)).wait_send()

    noise_g = Gather(along_col, nc, noise, noise_slot, ng_send, ng_recv, h, l)
    cut = cols * 3 // 8
    lat_span = (pl.ds(0, cut), pl.ds(cut, cols - cut))

    def lat_part(j, p):
        return lat_all.at[j, lat_span[p]]

    def lat_own(p):
        return lat.at[lat_span[p]]

    def lat_copy(kind, j, p, src=None):
        home = {"row": 2 * rh + cl, "col": col}
        side = {"row": 2 * rh + cl, "col": 2 * ch + 1 - cl}
        up = {"row": 2 * (rh + 1) + cl, "col": col}
        down = {"row": 2 * (rh - 1) + cl, "col": col}
        device = (home, side, up, down)[kind]
        return remote(
            lat_part(j, p) if src is None else src, lat_part(j, p),
            lg_send.at[kind, j, p], lg_recv.at[j, p], device,
        )

    def lat_relay(kind, j, p):
        device = (
            None, {"row": row, "col": 2 * ch + 1 - cl},
            {"row": row + 2, "col": col}, {"row": row - 2, "col": col},
        )[kind]
        return remote(lat_part(j, p), lat_part(j, p), lg_send.at[kind, j, p], lg_recv.at[j, p], device)

    def lat_arrived(j, p):
        lat_relay(1, j, p).wait_recv()

    def lat_side(act):
        for p in (1, 0):
            act(lat_copy(1, row, p, lat_own(p)))

    def lat_home(act):
        for p in (1, 0):
            act(lat_copy(0, row, p, lat_own(p)))

    def lat_line(act, p):
        @pl.when(rh < half_r - 1)
        def _():
            act(lat_copy(2, row, p, lat_own(p)))

        @pl.when(rh > 0)
        def _():
            act(lat_copy(3, row, p, lat_own(p)))

    def start(copy):
        copy.start()

    def wait_send(copy):
        copy.wait_send()

    def lat_pass(act, wait):
        @pl.when(turn)
        def _():
            for q in range(2):
                j = 2 * rh + q
                wait(j, 1)

                @pl.when(rh < half_r - 1)
                def _():
                    act(lat_relay(2, j, 1))

                @pl.when(rh > 0)
                def _():
                    act(lat_relay(3, j, 1))

        for s in range(1, half_r):
            for sign, kind in ((-1, 2), (1, 3)):
                k = rh + sign * s
                onward = (rh < half_r - 1) if sign < 0 else (rh > 0)
                valid = (k >= 0) if sign < 0 else (k < half_r)

                @pl.when(valid)
                def _():
                    for q in range(2):
                        j = 2 * k + q
                        if half_r > 2:
                            @pl.when(turn)
                            def _():
                                wait(j, 1)

                                @pl.when(onward)
                                def _():
                                    act(lat_relay(kind, j, 1))

                        @pl.when(jnp.logical_not(turn))
                        def _():
                            wait(j, 0)
                            act(lat_relay(1, j, 0))

                            @pl.when(onward)
                            def _():
                                act(lat_relay(kind, j, 0))
                                wait(j, 1)
                                act(lat_relay(kind, j, 1))

    def lat_ready(k):
        kh, kq = lax.div(k, 2), lax.rem(k, 2)
        near = kh == rh
        onward = ((kh < rh) & (rh < half_r - 1)) | ((kh > rh) & (rh > 0))

        @pl.when(turn)
        def _():
            lat_arrived(k, 0)
            if half_r == 2:
                @pl.when(jnp.logical_not(near))
                def _():
                    lat_arrived(k, 1)

        @pl.when(jnp.logical_not(turn) & near & (kq != rl))
        def _():
            lat_arrived(k, 0)
            lat_arrived(k, 1)

        @pl.when(jnp.logical_not(turn) & jnp.logical_not(near) & jnp.logical_not(onward))
        def _():
            lat_arrived(k, 1)

    noise_swap = remote(noise, turned, swap_send.at[0], swap_recv.at[0], across)

    @pl.when(turn)
    def _():
        noise_swap.start()

    @pl.when(jnp.logical_not(turn))
    def _():
        noise_g.first()

    lat_line(start, 0)
    keep_noise = pltpu.make_async_copy(noise, noise_slot(c), local_sem.at[0])
    keep_turned = pltpu.make_async_copy(turned, noise_slot(c), local_sem.at[0])
    keep_lat = pltpu.make_async_copy(lat, lat_all.at[row], local_sem.at[1])

    @pl.when(jnp.logical_not(turn))
    def _():
        keep_noise.start()
        keep_lat.start()

    @pl.when(turn)
    def _():
        noise_swap.wait_recv()
        noise_g.own = turned
        noise_g.first()
        lat_side(start)
        keep_turned.start()
        lat_home(start)

    colp[...] = jnp.zeros_like(colp)

    tile_n = min(256, cols)

    def block(k, add):
        @pl.loop(0, cols // tile_n)
        def _(t):
            span = pl.ds(pl.multiple_of(t * tile_n, tile_n), tile_n)
            part = lax.dot_general(
                noise_all[k], lat_all[k, span, :], (((1,), (1,)), ((), ())),
                preferred_element_type=jnp.float32,
            ) * scale
            if add:
                logits[:, span] += part
            else:
                logits[:, span] = part

    def noise_ready(k):
        noise_g.other(k)

    noise_g.forward(1)

    @pl.when(jnp.logical_not(turn))
    def _():
        lat_side(start)

    lat_line(wait_send, 0)
    lat_line(start, 1)
    lat_pass(start, lat_arrived)
    for s in range(2, hi - 1):
        noise_g.forward(s)

    @pl.when(jnp.logical_not(turn))
    def _():
        keep_noise.wait()
        keep_lat.wait()

    @pl.when(turn)
    def _():
        keep_turned.wait()

    near = jnp.minimum(jnp.maximum(h, 2 * rh), 2 * rh + 1)
    noise_ready(near)
    lat_ready(near)
    block(near, False)
    if hi > 2:
        noise_g.forward(hi - 1)

    @pl.loop(1, hi)
    def _(i):
        k = jnp.where(i == 1, 4 * rh + 1 - near, lax.rem(2 * rh + i, hi))
        noise_ready(k)
        lat_ready(k)
        block(k, True)

    def exchange(along, n, me, box, send, recv):
        for d in range(1, n):
            remote(box.at[me], box.at[me], send.at[d], recv.at[me], along(lax.rem(me + d, n))).start()
        for d in range(1, n):
            j = lax.rem(me + n - d, n)
            remote(box.at[j], box.at[j], send.at[d], recv.at[j], along(j)).wait_recv()

    def sent(along, n, me, box, send, recv):
        for d in range(1, n):
            remote(box.at[me], box.at[me], send.at[d], recv.at[me], along(lax.rem(me + d, n))).wait_send()

    def merged(n, box):
        high = functools.reduce(jnp.maximum, [box[j, 0:1, :] for j in range(n)])
        total = functools.reduce(
            jnp.add, [box[j, 1:2, :] * jnp.exp(box[j, 0:1, :] - high) for j in range(n)]
        )
        return high + jnp.log(total)

    def lane(g):
        return pl.ds(g * LANES, LANES)

    row_tile = 32
    col_tile = 64

    for step in range(ITERS):
        @pl.loop(0, rows // row_tile, unroll=2)
        def _(t):
            span = pl.ds(pl.multiple_of(t * row_tile, row_tile), row_tile)
            v = [logits[span, lane(g)] + colp[:, lane(g)] for g in range(groups)]
            m = functools.reduce(jnp.maximum, v)
            mt[span, :] = m
            st[span, :] = functools.reduce(jnp.add, [jnp.exp(x - m) for x in v])

        m = mt[...].T
        high = jnp.max(m, axis=0, keepdims=True)
        box = row_box.at[step]
        mine_box = box.at[c]
        mine_box[0:1, :] = high
        mine_box[1:2, :] = jnp.sum(st[...].T * jnp.exp(m - high), axis=0, keepdims=True)
        exchange(along_col, nc, c, box, row_send.at[step], row_recv.at[step])
        rowp = -math.log(rows * nr) - merged(nc, box)
        row_swap[0] = rowp
        rowb[...] = jnp.broadcast_to(rowp, (LANES, rows)).T

        @pl.loop(0, rows // col_tile)
        def _(t):
            span = pl.ds(pl.multiple_of(t * col_tile, col_tile), col_tile)
            small = pl.ds(pl.multiple_of(t * 8, 8), 8)
            shift = rowb[span, :]
            for g in range(groups):
                v = (logits[span, lane(g)] + shift).reshape(col_tile // 8, 8, LANES)
                m = jnp.max(v, axis=0)
                mc[small, lane(g)] = m
                sc[small, lane(g)] = jnp.sum(jnp.exp(v - m[None]), axis=0)

        m = mc[...]
        high = jnp.max(m, axis=0, keepdims=True)
        box = col_box.at[step]
        mine_box = box.at[r]
        mine_box[0:1, :] = high
        mine_box[1:2, :] = jnp.sum(sc[...] * jnp.exp(m - high), axis=0, keepdims=True)
        exchange(along_row, nr, r, box, col_send.at[step], col_recv.at[step])
        colp[...] = -math.log(cols * nc) - merged(nr, box)
    row_pair = remote(row_swap.at[0], row_swap.at[1], swap_send.at[1], swap_recv.at[1], across)
    col_pair = remote(colp, col_swap, swap_send.at[2], swap_recv.at[2], across)

    @pl.when(turn)
    def _():
        row_pair.start()
        col_pair.start()

    @pl.when(jnp.logical_not(turn))
    def _():
        row_out[...] = row_swap[0]
        col_out[...] = colp[...]


    @pl.loop(0, rows // row_tile, unroll=2)
    def _(t):
        span = pl.ds(pl.multiple_of(t * row_tile, row_tile), row_tile)
        shift = rowb[span, :]
        total = jnp.zeros((row_tile, LANES), jnp.float32)
        for g in range(groups):
            p = jnp.exp(logits[span, lane(g)] + shift + colp[:, lane(g)]).astype(jnp.bfloat16)
            plan[span, lane(g)] = p
            total += p.astype(jnp.float32)
        mt[span, :] = total

    tile_k = min(256, kn)

    parts = 4
    part = rows // parts
    add_tile = min(128, part)

    def rows_of(p):
        return pl.ds(pl.multiple_of(p * part, part), part)

    def share(k, side, p, dst):
        @pl.loop(0, kn // tile_k)
        def _(t):
            off = pl.multiple_of(t * tile_k, tile_k)
            src = pl.multiple_of(side * kn + t * tile_k, tile_k)
            dst[k, rows_of(p), pl.ds(off, tile_k)] = jnp.dot(
                plan[rows_of(p), :], lat_all[k, :, pl.ds(src, tile_k)], preferred_element_type=jnp.float32
            ).astype(jnp.bfloat16)

    def piece(ref, k, p):
        return ref.at[k, rows_of(p)]

    def x_copy(k, p):
        return remote(
            piece(x_send, k, p), piece(x_recv, k, p), xs_sem.at[k, p], xr_sem.at[k, p],
            along_col(c + 1 - 2 * l),
        )

    def up_copy(k, p):
        return remote(
            piece(own, k, p), piece(z_low, k, p), up_sem.at[k, p], low_sem.at[k, p], along_col(c + 2)
        )

    def down_copy(k, p):
        return remote(
            piece(own, k, p), piece(z_high, k, p), down_sem.at[k, p], high_sem.at[k, p], along_col(c - 2)
        )

    def farthest_first(body):
        @pl.loop(0, 2 * hi - 1)
        def _(p):
            s = hi - 1 - lax.div(p, 2)
            k = h + s * (1 - 2 * lax.rem(p, 2))

            @pl.when((k >= 0) & (k < hi))
            def _():
                body(k)

    f32, bf16 = jnp.float32, jnp.bfloat16

    def tiles(p, body):
        @pl.loop(0, part // add_tile)
        def _(t):
            body(pl.ds(pl.multiple_of(p * part + t * add_tile, add_tile), add_tile))

    def add(k, p, third):
        def body(span):
            total = own[k, span, :].astype(f32) + third[k, span, :].astype(f32)
            own[k, span, :] = total.astype(bf16)
        tiles(p, body)

    def work(k):
        @pl.loop(0, parts)
        def _(p):
            share(k, 1 - l, p, x_send)
            x_copy(k, p).start()

        @pl.loop(0, parts)
        def _(p):
            share(k, l, p, own)
            x_copy(k, p).wait_recv()
            add(k, p, x_recv)

            @pl.when((k > h) & (h == 0))
            def _():
                up_copy(k, p).start()

            @pl.when((k < h) & (h == hi - 1))
            def _():
                down_copy(k, p).start()

    farthest_first(work)

    mine_box = row_box.at[ITERS, c]
    mine_box[0:1, :] = jnp.sum(mt[...].T, axis=0, keepdims=True)
    mine_box[1:2, :] = jnp.zeros((1, rows), f32)
    exchange(along_col, nc, c, row_box.at[ITERS], row_send.at[ITERS], row_recv.at[ITERS])
    mass = functools.reduce(jnp.add, [row_box[ITERS, j, 0:1, :] for j in range(nc)])
    rowb[...] = jnp.broadcast_to(1.0 / mass, (LANES, rows)).T

    def relay(k):
        @pl.loop(0, parts)
        def _(p):
            @pl.when((k > h) & (h > 0))
            def _():
                up_copy(k, p).wait_recv()
                add(k, p, z_low)
                up_copy(k, p).start()

            @pl.when((k < h) & (h < hi - 1))
            def _():
                down_copy(k, p).wait_recv()
                add(k, p, z_high)
                down_copy(k, p).start()

    farthest_first(relay)

    def out_copy(p):
        span = rows_of(p)
        return remote(result.at[span], out_box.at[span], out_send.at[p], out_recv.at[p], across)

    @pl.loop(0, parts)
    def _(p):
        def start_sum(span):
            num[span, :] = own[h, span, :].astype(f32)

        tiles(p, start_sum)

        def add_low(span):
            num[span, :] += z_low[h, span, :].astype(f32)

        def add_high(span):
            num[span, :] += z_high[h, span, :].astype(f32)

        @pl.when(h > 0)
        def _():
            up_copy(h, p).wait_recv()
            tiles(p, add_low)

        @pl.when(h < hi - 1)
        def _():
            down_copy(h, p).wait_recv()
            tiles(p, add_high)

        def divide(ref):
            def body(span):
                inverse = rowb[span, :]
                for g in range(kn // LANES):
                    ref[span, lane(g)] = (num[span, lane(g)] * inverse).astype(bf16)
            tiles(p, body)

        @pl.when(turn)
        def _():
            divide(result)
            out_copy(p).start()

        @pl.when(jnp.logical_not(turn))
        def _():
            divide(out)

    @pl.when(turn)
    def _():
        row_pair.wait()
        col_pair.wait()
        row_out[...] = row_swap[1]
        col_out[...] = col_swap[...]
        for p in range(parts):
            out_copy(p).wait_recv()

            def body(span):
                out[span, :] = out_box[span, :]
            tiles(p, body)
        for p in range(parts):
            out_copy(p).wait_send()
        noise_swap.wait_send()

    noise_g.finish()
    lat_side(wait_send)
    lat_line(wait_send, 1)

    @pl.when(turn)
    def _():
        lat_home(wait_send)

    lat_pass(wait_send, lambda j, p: None)
    for step in range(ITERS + 1):
        sent(along_col, nc, c, row_box.at[step], row_send.at[step], row_recv.at[step])
    for step in range(ITERS):
        sent(along_row, nr, r, col_box.at[step], col_send.at[step], col_recv.at[step])

    @pl.loop(0, hi)
    def _(k):
        @pl.loop(0, parts)
        def _(p):
            x_copy(k, p).wait_send()

            @pl.when(k > h)
            def _():
                up_copy(k, p).wait_send()

            @pl.when(k < h)
            def _():
                down_copy(k, p).wait_send()


def on_device(nr, nc, noise, latents):
    rows, kn = noise.shape
    cols, kl = latents.shape
    hi = nc // 2
    bf16, f32 = jnp.bfloat16, jnp.float32
    vmem, dma = pltpu.VMEM, pltpu.SemaphoreType.DMA
    transported, row_potential, col_potential = pl.pallas_call(
        functools.partial(kernel, nr, nc),
        out_shape=(
            jax.ShapeDtypeStruct((rows, kn), bf16),
            jax.ShapeDtypeStruct((1, rows), f32),
            jax.ShapeDtypeStruct((1, cols), f32),
        ),
        in_specs=[pl.BlockSpec(memory_space=pl.ANY)] * 2,
        out_specs=[pl.BlockSpec(memory_space=pltpu.VMEM)] * 3,
        scratch_shapes=[
            vmem((hi, rows, 2 * kn), bf16),
            vmem((nr, cols, kl), bf16),
            vmem((rows, cols), f32),
            vmem((rows, cols), bf16),
            vmem((rows, LANES), f32),
            vmem((rows, LANES), f32),
            vmem((rows, LANES), f32),
            vmem((rows // 8, cols), f32),
            vmem((rows // 8, cols), f32),
            vmem((1, cols), f32),
            vmem((ITERS + 1, nc, 2, rows), f32),
            vmem((ITERS, nr, 2, cols), f32),
            vmem((hi, rows, kn), bf16),
            vmem((hi, rows, kn), bf16),
            vmem((hi, rows, kn), bf16),
            vmem((hi, rows, kn), bf16),
            vmem((hi, rows, kn), bf16),
            vmem((rows, kn), f32),
            vmem((rows, kn), bf16),
            vmem((rows, kn), bf16),
            vmem((rows, kn), bf16),
            vmem((2, 1, rows), f32),
            vmem((1, cols), f32),
            dma((2,)),
            dma((3, hi)), dma((nc,)),
            dma((4, nr, 2)), dma((nr, 2)),
            dma((ITERS + 1, nc)), dma((ITERS + 1, nc)),
            dma((ITERS, nr)), dma((ITERS, nr)),
            dma((hi, 4)), dma((hi, 4)), dma((hi, 4)), dma((hi, 4)), dma((hi, 4)), dma((hi, 4)),
            dma((3,)), dma((3,)), dma((4,)), dma((4,)),
        ],
        compiler_params=pltpu.CompilerParams(
            collective_id=0, has_side_effects=True, vmem_limit_bytes=58 * 2**20
        ),
        cost_estimate=pl.CostEstimate(
            flops=4 * rows * cols * kl * nr, bytes_accessed=8 * 2**20, transcendentals=7 * rows * cols
        ),
    )(noise, latents)
    return transported, row_potential.reshape(rows), col_potential.reshape(cols)


def solution(mesh):
    in_specs = (P("row", "col"), P("col", "row"))
    out_specs = (P("row", "col"), P("row"), P("col"))
    return jax.shard_map(
        functools.partial(on_device, mesh.shape["row"], mesh.shape["col"]),
        mesh=mesh, in_specs=in_specs, out_specs=out_specs, check_vma=False,
    )
```

```python
import functools
import math

import jax
import jax.numpy as jnp
from jax import lax
from jax.experimental import pallas as pl
from jax.experimental.pallas import tpu as pltpu
from jax.sharding import PartitionSpec as P

ITERS = 3
EPSILON = 0.01
LANES = 128
MESH = pl.DeviceIdType.MESH


def kernel(
    nr, nc, noise, lat,
    out, row_out, col_out,
    noise_all, lat_all, logits, plan, rowb, mt, st, mc, sc, colp,
    row_box, col_box, x_send, x_recv, own, z_low, z_high, num, turned, result, out_box, row_swap, col_swap,
    local_sem, ng_send, ng_recv, lg_send, lg_recv,
    row_send, row_recv, col_send, col_recv,
    xs_sem, xr_sem, up_sem, low_sem, down_sem, high_sem, swap_send, swap_recv, out_send, out_recv,
):
    rows, kn = noise.shape
    cols, kl = lat.shape
    width = kl * nr
    hi = nc // 2
    groups = cols // LANES
    scale = 2.0 / (width * EPSILON)
    row = lax.axis_index("row")
    col = lax.axis_index("col")
    ch, cl = lax.div(col, 2), lax.rem(col, 2)
    rh, rl = lax.div(row, 2), lax.rem(row, 2)
    r, c = 2 * rh + cl, 2 * ch + rl
    h, l = ch, rl
    turn = rl != cl
    half_r = nr // 2

    def along_col(j):
        return {"row": 2 * rh + lax.rem(j, 2), "col": 2 * lax.div(j, 2) + cl}

    def along_row(j):
        return {"row": 2 * lax.div(j, 2) + rl, "col": 2 * ch + lax.rem(j, 2)}

    across = {"row": 2 * rh + 1 - rl, "col": 2 * ch + 1 - cl}

    barrier = pltpu.get_barrier_semaphore()

    def greet(device):
        pl.semaphore_signal(barrier, inc=1, device_id=device, device_id_type=MESH)

    for d in range(1, nc):
        greet(along_col(lax.rem(c + d, nc)))
    for d in range(1, nr):
        greet(along_row(lax.rem(r + d, nr)))
    for d in range(1, half_r):
        greet({"row": 2 * lax.rem(rh + d, half_r) + 1 - rl, "col": col})
    greet(across)
    pl.semaphore_wait(barrier, nc - 1 + nr - 1 + half_r - 1 + 1)

    def noise_slot(j):
        return noise_all.at[lax.div(j, 2), :, pl.ds(pl.multiple_of(lax.rem(j, 2) * kn, kn), kn)]

    def remote(src, dst, send, recv, device):
        return pltpu.make_async_remote_copy(
            src_ref=src, dst_ref=dst, send_sem=send, recv_sem=recv,
            device_id=device, device_id_type=MESH,
        )

    class Gather:
        def __init__(self, along, n, own_ref, slot, send, recv, ah, al):
            self.along, self.half, self.own, self.slot = along, n // 2, own_ref, slot
            self.send, self.recv, self.h, self.l = send, recv, ah, al
            self.me = 2 * ah + al

        def copy(self, kind, j, src):
            target = (self.me + 1 - 2 * self.l, self.me + 2, self.me - 2)[kind]
            return remote(
                src, self.slot(j), self.send.at[kind, lax.div(j, 2)], self.recv.at[j], self.along(target)
            )

        def first(self):
            @pl.when(self.h < self.half - 1)
            def _():
                self.copy(1, self.me, self.own).start()

            @pl.when(self.h > 0)
            def _():
                self.copy(2, self.me, self.own).start()

            self.copy(0, self.me, self.own).start()

        def arrived(self, j):
            self.copy(0, j, self.slot(j)).wait_recv()

        def forward(self, s):
            @pl.when(self.h - s >= 0)
            def _():
                j = self.me - 2 * s
                self.arrived(j)

                @pl.when(self.h < self.half - 1)
                def _():
                    self.copy(1, j, self.slot(j)).start()

                self.copy(0, j, self.slot(j)).start()

            @pl.when(self.h + s < self.half)
            def _():
                j = self.me + 2 * s
                self.arrived(j)

                @pl.when(self.h > 0)
                def _():
                    self.copy(2, j, self.slot(j)).start()

                self.copy(0, j, self.slot(j)).start()

        def other(self, k):
            self.arrived(2 * k + 1 - self.l)

        def finish(self):
            @pl.loop(0, self.half)
            def _(k):
                j = 2 * k + self.l
                self.copy(0, j, self.slot(j)).wait_send()

                @pl.when((k <= self.h) & (self.h < self.half - 1))
                def _():
                    self.copy(1, j, self.slot(j)).wait_send()

                @pl.when((k >= self.h) & (self.h > 0))
                def _():
                    self.copy(2, j, self.slot(j)).wait_send()

    noise_g = Gather(along_col, nc, noise, noise_slot, ng_send, ng_recv, h, l)
    cut = cols * 3 // 8
    lat_span = (pl.ds(0, cut), pl.ds(cut, cols - cut))

    def lat_part(j, p):
        return lat_all.at[j, lat_span[p]]

    def lat_own(p):
        return lat.at[lat_span[p]]

    def lat_copy(kind, j, p, src=None):
        home = {"row": 2 * rh + cl, "col": col}
        side = {"row": 2 * rh + cl, "col": 2 * ch + 1 - cl}
        up = {"row": 2 * (rh + 1) + cl, "col": col}
        down = {"row": 2 * (rh - 1) + cl, "col": col}
        device = (home, side, up, down)[kind]
        return remote(
            lat_part(j, p) if src is None else src, lat_part(j, p),
            lg_send.at[kind, j, p], lg_recv.at[j, p], device,
        )

    def lat_relay(kind, j, p):
        device = (
            None, {"row": row, "col": 2 * ch + 1 - cl},
            {"row": row + 2, "col": col}, {"row": row - 2, "col": col},
        )[kind]
        return remote(lat_part(j, p), lat_part(j, p), lg_send.at[kind, j, p], lg_recv.at[j, p], device)

    def lat_arrived(j, p):
        lat_relay(1, j, p).wait_recv()

    def lat_side(act):
        for p in (1, 0):
            act(lat_copy(1, row, p, lat_own(p)))

    def lat_home(act):
        for p in (1, 0):
            act(lat_copy(0, row, p, lat_own(p)))

    def lat_line(act, p):
        @pl.when(rh < half_r - 1)
        def _():
            act(lat_copy(2, row, p, lat_own(p)))

        @pl.when(rh > 0)
        def _():
            act(lat_copy(3, row, p, lat_own(p)))

    def start(copy):
        copy.start()

    def wait_send(copy):
        copy.wait_send()

    def lat_pass(act, wait):
        @pl.when(turn)
        def _():
            for q in range(2):
                j = 2 * rh + q
                wait(j, 1)

                @pl.when(rh < half_r - 1)
                def _():
                    act(lat_relay(2, j, 1))

                @pl.when(rh > 0)
                def _():
                    act(lat_relay(3, j, 1))

        for s in range(1, half_r):
            for sign, kind in ((-1, 2), (1, 3)):
                k = rh + sign * s
                onward = (rh < half_r - 1) if sign < 0 else (rh > 0)
                valid = (k >= 0) if sign < 0 else (k < half_r)

                @pl.when(valid)
                def _():
                    for q in range(2):
                        j = 2 * k + q
                        if half_r > 2:
                            @pl.when(turn)
                            def _():
                                wait(j, 1)

                                @pl.when(onward)
                                def _():
                                    act(lat_relay(kind, j, 1))

                        @pl.when(jnp.logical_not(turn))
                        def _():
                            wait(j, 0)
                            act(lat_relay(1, j, 0))

                            @pl.when(onward)
                            def _():
                                act(lat_relay(kind, j, 0))
                                wait(j, 1)
                                act(lat_relay(kind, j, 1))

    def lat_ready(k):
        kh, kq = lax.div(k, 2), lax.rem(k, 2)
        near = kh == rh
        onward = ((kh < rh) & (rh < half_r - 1)) | ((kh > rh) & (rh > 0))

        @pl.when(turn)
        def _():
            lat_arrived(k, 0)
            if half_r == 2:
                @pl.when(jnp.logical_not(near))
                def _():
                    lat_arrived(k, 1)

        @pl.when(jnp.logical_not(turn) & near & (kq != rl))
        def _():
            lat_arrived(k, 0)
            lat_arrived(k, 1)

        @pl.when(jnp.logical_not(turn) & jnp.logical_not(near) & jnp.logical_not(onward))
        def _():
            lat_arrived(k, 1)

    noise_swap = remote(noise, turned, swap_send.at[0], swap_recv.at[0], across)

    @pl.when(turn)
    def _():
        noise_swap.start()

    @pl.when(jnp.logical_not(turn))
    def _():
        noise_g.first()

    lat_line(start, 0)
    lat_line(start, 1)
    keep_noise = pltpu.make_async_copy(noise, noise_slot(c), local_sem.at[0])
    keep_turned = pltpu.make_async_copy(turned, noise_slot(c), local_sem.at[0])
    keep_lat = pltpu.make_async_copy(lat, lat_all.at[row], local_sem.at[1])

    @pl.when(jnp.logical_not(turn))
    def _():
        keep_noise.start()
        keep_lat.start()

    @pl.when(turn)
    def _():
        noise_swap.wait_recv()
        noise_g.own = turned
        noise_g.first()
        lat_side(start)
        keep_turned.start()
        lat_home(start)

    colp[...] = jnp.zeros_like(colp)

    tile_n = min(256, cols)

    def block(k, add):
        @pl.loop(0, cols // tile_n)
        def _(t):
            span = pl.ds(pl.multiple_of(t * tile_n, tile_n), tile_n)
            part = lax.dot_general(
                noise_all[k], lat_all[k, span, :], (((1,), (1,)), ((), ())),
                preferred_element_type=jnp.float32,
            ) * scale
            if add:
                logits[:, span] += part
            else:
                logits[:, span] = part

    def noise_ready(k):
        noise_g.other(k)

    noise_g.forward(1)

    @pl.when(jnp.logical_not(turn))
    def _():
        lat_side(start)

    for s in range(2, hi - 1):
        noise_g.forward(s)
    lat_pass(start, lat_arrived)

    @pl.when(jnp.logical_not(turn))
    def _():
        keep_noise.wait()
        keep_lat.wait()

    @pl.when(turn)
    def _():
        keep_turned.wait()

    near = jnp.minimum(jnp.maximum(h, 2 * rh), 2 * rh + 1)
    noise_ready(near)
    lat_ready(near)
    block(near, False)
    if hi > 2:
        noise_g.forward(hi - 1)

    @pl.loop(1, hi)
    def _(i):
        k = jnp.where(i == 1, 4 * rh + 1 - near, lax.rem(2 * rh + i, hi))
        noise_ready(k)
        lat_ready(k)
        block(k, True)

    def exchange(along, n, me, box, send, recv):
        for d in range(1, n):
            remote(box.at[me], box.at[me], send.at[d], recv.at[me], along(lax.rem(me + d, n))).start()
        for d in range(1, n):
            j = lax.rem(me + n - d, n)
            remote(box.at[j], box.at[j], send.at[d], recv.at[j], along(j)).wait_recv()

    def sent(along, n, me, box, send, recv):
        for d in range(1, n):
            remote(box.at[me], box.at[me], send.at[d], recv.at[me], along(lax.rem(me + d, n))).wait_send()

    def merged(n, box):
        high = functools.reduce(jnp.maximum, [box[j, 0:1, :] for j in range(n)])
        total = functools.reduce(
            jnp.add, [box[j, 1:2, :] * jnp.exp(box[j, 0:1, :] - high) for j in range(n)]
        )
        return high + jnp.log(total)

    def lane(g):
        return pl.ds(g * LANES, LANES)

    row_tile = 32
    col_tile = 64

    for step in range(ITERS):
        @pl.loop(0, rows // row_tile, unroll=2)
        def _(t):
            span = pl.ds(pl.multiple_of(t * row_tile, row_tile), row_tile)
            v = [logits[span, lane(g)] + colp[:, lane(g)] for g in range(groups)]
            m = functools.reduce(jnp.maximum, v)
            mt[span, :] = m
            st[span, :] = functools.reduce(jnp.add, [jnp.exp(x - m) for x in v])

        m = mt[...].T
        high = jnp.max(m, axis=0, keepdims=True)
        box = row_box.at[step]
        mine_box = box.at[c]
        mine_box[0:1, :] = high
        mine_box[1:2, :] = jnp.sum(st[...].T * jnp.exp(m - high), axis=0, keepdims=True)
        exchange(along_col, nc, c, box, row_send.at[step], row_recv.at[step])
        rowp = -math.log(rows * nr) - merged(nc, box)
        row_swap[0] = rowp
        rowb[...] = jnp.broadcast_to(rowp, (LANES, rows)).T

        @pl.loop(0, rows // col_tile)
        def _(t):
            span = pl.ds(pl.multiple_of(t * col_tile, col_tile), col_tile)
            small = pl.ds(pl.multiple_of(t * 8, 8), 8)
            shift = rowb[span, :]
            for g in range(groups):
                v = (logits[span, lane(g)] + shift).reshape(col_tile // 8, 8, LANES)
                m = jnp.max(v, axis=0)
                mc[small, lane(g)] = m
                sc[small, lane(g)] = jnp.sum(jnp.exp(v - m[None]), axis=0)

        m = mc[...]
        high = jnp.max(m, axis=0, keepdims=True)
        box = col_box.at[step]
        mine_box = box.at[r]
        mine_box[0:1, :] = high
        mine_box[1:2, :] = jnp.sum(sc[...] * jnp.exp(m - high), axis=0, keepdims=True)
        exchange(along_row, nr, r, box, col_send.at[step], col_recv.at[step])
        colp[...] = -math.log(cols * nc) - merged(nr, box)
    row_pair = remote(row_swap.at[0], row_swap.at[1], swap_send.at[1], swap_recv.at[1], across)
    col_pair = remote(colp, col_swap, swap_send.at[2], swap_recv.at[2], across)

    @pl.when(turn)
    def _():
        row_pair.start()
        col_pair.start()

    @pl.when(jnp.logical_not(turn))
    def _():
        row_out[...] = row_swap[0]
        col_out[...] = colp[...]


    @pl.loop(0, rows // row_tile, unroll=2)
    def _(t):
        span = pl.ds(pl.multiple_of(t * row_tile, row_tile), row_tile)
        shift = rowb[span, :]
        total = jnp.zeros((row_tile, LANES), jnp.float32)
        for g in range(groups):
            p = jnp.exp(logits[span, lane(g)] + shift + colp[:, lane(g)]).astype(jnp.bfloat16)
            plan[span, lane(g)] = p
            total += p.astype(jnp.float32)
        mt[span, :] = total

    tile_k = min(256, kn)

    parts = 4
    part = rows // parts
    add_tile = min(128, part)

    def rows_of(p):
        return pl.ds(pl.multiple_of(p * part, part), part)

    def share(k, side, p, dst):
        @pl.loop(0, kn // tile_k)
        def _(t):
            off = pl.multiple_of(t * tile_k, tile_k)
            src = pl.multiple_of(side * kn + t * tile_k, tile_k)
            dst[k, rows_of(p), pl.ds(off, tile_k)] = jnp.dot(
                plan[rows_of(p), :], lat_all[k, :, pl.ds(src, tile_k)], preferred_element_type=jnp.float32
            ).astype(jnp.bfloat16)

    def piece(ref, k, p):
        return ref.at[k, rows_of(p)]

    def x_copy(k, p):
        return remote(
            piece(x_send, k, p), piece(x_recv, k, p), xs_sem.at[k, p], xr_sem.at[k, p],
            along_col(c + 1 - 2 * l),
        )

    def up_copy(k, p):
        return remote(
            piece(own, k, p), piece(z_low, k, p), up_sem.at[k, p], low_sem.at[k, p], along_col(c + 2)
        )

    def down_copy(k, p):
        return remote(
            piece(own, k, p), piece(z_high, k, p), down_sem.at[k, p], high_sem.at[k, p], along_col(c - 2)
        )

    def farthest_first(body):
        @pl.loop(0, 2 * hi - 1)
        def _(p):
            s = hi - 1 - lax.div(p, 2)
            k = h + s * (1 - 2 * lax.rem(p, 2))

            @pl.when((k >= 0) & (k < hi))
            def _():
                body(k)

    f32, bf16 = jnp.float32, jnp.bfloat16

    def tiles(p, body):
        @pl.loop(0, part // add_tile)
        def _(t):
            body(pl.ds(pl.multiple_of(p * part + t * add_tile, add_tile), add_tile))

    def add(k, p, third):
        def body(span):
            total = own[k, span, :].astype(f32) + third[k, span, :].astype(f32)
            own[k, span, :] = total.astype(bf16)
        tiles(p, body)

    def work(k):
        @pl.loop(0, parts)
        def _(p):
            share(k, 1 - l, p, x_send)
            x_copy(k, p).start()

        @pl.loop(0, parts)
        def _(p):
            share(k, l, p, own)
            x_copy(k, p).wait_recv()
            add(k, p, x_recv)

            @pl.when((k > h) & (h == 0))
            def _():
                up_copy(k, p).start()

            @pl.when((k < h) & (h == hi - 1))
            def _():
                down_copy(k, p).start()

    farthest_first(work)

    mine_box = row_box.at[ITERS, c]
    mine_box[0:1, :] = jnp.sum(mt[...].T, axis=0, keepdims=True)
    mine_box[1:2, :] = jnp.zeros((1, rows), f32)
    exchange(along_col, nc, c, row_box.at[ITERS], row_send.at[ITERS], row_recv.at[ITERS])
    mass = functools.reduce(jnp.add, [row_box[ITERS, j, 0:1, :] for j in range(nc)])
    rowb[...] = jnp.broadcast_to(1.0 / mass, (LANES, rows)).T

    def relay(k):
        @pl.loop(0, parts)
        def _(p):
            @pl.when((k > h) & (h > 0))
            def _():
                up_copy(k, p).wait_recv()
                add(k, p, z_low)
                up_copy(k, p).start()

            @pl.when((k < h) & (h < hi - 1))
            def _():
                down_copy(k, p).wait_recv()
                add(k, p, z_high)
                down_copy(k, p).start()

    farthest_first(relay)

    def out_copy(p):
        span = rows_of(p)
        return remote(result.at[span], out_box.at[span], out_send.at[p], out_recv.at[p], across)

    @pl.loop(0, parts)
    def _(p):
        def start_sum(span):
            num[span, :] = own[h, span, :].astype(f32)

        tiles(p, start_sum)

        def add_low(span):
            num[span, :] += z_low[h, span, :].astype(f32)

        def add_high(span):
            num[span, :] += z_high[h, span, :].astype(f32)

        @pl.when(h > 0)
        def _():
            up_copy(h, p).wait_recv()
            tiles(p, add_low)

        @pl.when(h < hi - 1)
        def _():
            down_copy(h, p).wait_recv()
            tiles(p, add_high)

        def divide(ref):
            def body(span):
                inverse = rowb[span, :]
                for g in range(kn // LANES):
                    ref[span, lane(g)] = (num[span, lane(g)] * inverse).astype(bf16)
            tiles(p, body)

        @pl.when(turn)
        def _():
            divide(result)
            out_copy(p).start()

        @pl.when(jnp.logical_not(turn))
        def _():
            divide(out)

    @pl.when(turn)
    def _():
        row_pair.wait()
        col_pair.wait()
        row_out[...] = row_swap[1]
        col_out[...] = col_swap[...]
        for p in range(parts):
            out_copy(p).wait_recv()

            def body(span):
                out[span, :] = out_box[span, :]
            tiles(p, body)
        for p in range(parts):
            out_copy(p).wait_send()
        noise_swap.wait_send()

    noise_g.finish()
    lat_side(wait_send)
    lat_line(wait_send, 0)
    lat_line(wait_send, 1)

    @pl.when(turn)
    def _():
        lat_home(wait_send)

    lat_pass(wait_send, lambda j, p: None)
    for step in range(ITERS + 1):
        sent(along_col, nc, c, row_box.at[step], row_send.at[step], row_recv.at[step])
    for step in range(ITERS):
        sent(along_row, nr, r, col_box.at[step], col_send.at[step], col_recv.at[step])

    @pl.loop(0, hi)
    def _(k):
        @pl.loop(0, parts)
        def _(p):
            x_copy(k, p).wait_send()

            @pl.when(k > h)
            def _():
                up_copy(k, p).wait_send()

            @pl.when(k < h)
            def _():
                down_copy(k, p).wait_send()


def on_device(nr, nc, noise, latents):
    rows, kn = noise.shape
    cols, kl = latents.shape
    hi = nc // 2
    bf16, f32 = jnp.bfloat16, jnp.float32
    vmem, dma = pltpu.VMEM, pltpu.SemaphoreType.DMA
    transported, row_potential, col_potential = pl.pallas_call(
        functools.partial(kernel, nr, nc),
        out_shape=(
            jax.ShapeDtypeStruct((rows, kn), bf16),
            jax.ShapeDtypeStruct((1, rows), f32),
            jax.ShapeDtypeStruct((1, cols), f32),
        ),
        in_specs=[pl.BlockSpec(memory_space=pl.ANY)] * 2,
        out_specs=[pl.BlockSpec(memory_space=pltpu.VMEM)] * 3,
        scratch_shapes=[
            vmem((hi, rows, 2 * kn), bf16),
            vmem((nr, cols, kl), bf16),
            vmem((rows, cols), f32),
            vmem((rows, cols), bf16),
            vmem((rows, LANES), f32),
            vmem((rows, LANES), f32),
            vmem((rows, LANES), f32),
            vmem((rows // 8, cols), f32),
            vmem((rows // 8, cols), f32),
            vmem((1, cols), f32),
            vmem((ITERS + 1, nc, 2, rows), f32),
            vmem((ITERS, nr, 2, cols), f32),
            vmem((hi, rows, kn), bf16),
            vmem((hi, rows, kn), bf16),
            vmem((hi, rows, kn), bf16),
            vmem((hi, rows, kn), bf16),
            vmem((hi, rows, kn), bf16),
            vmem((rows, kn), f32),
            vmem((rows, kn), bf16),
            vmem((rows, kn), bf16),
            vmem((rows, kn), bf16),
            vmem((2, 1, rows), f32),
            vmem((1, cols), f32),
            dma((2,)),
            dma((3, hi)), dma((nc,)),
            dma((4, nr, 2)), dma((nr, 2)),
            dma((ITERS + 1, nc)), dma((ITERS + 1, nc)),
            dma((ITERS, nr)), dma((ITERS, nr)),
            dma((hi, 4)), dma((hi, 4)), dma((hi, 4)), dma((hi, 4)), dma((hi, 4)), dma((hi, 4)),
            dma((3,)), dma((3,)), dma((4,)), dma((4,)),
        ],
        compiler_params=pltpu.CompilerParams(
            collective_id=0, has_side_effects=True, vmem_limit_bytes=58 * 2**20
        ),
        cost_estimate=pl.CostEstimate(
            flops=4 * rows * cols * kl * nr, bytes_accessed=8 * 2**20, transcendentals=7 * rows * cols
        ),
    )(noise, latents)
    return transported, row_potential.reshape(rows), col_potential.reshape(cols)


def solution(mesh):
    in_specs = (P("row", "col"), P("col", "row"))
    out_specs = (P("row", "col"), P("row"), P("col"))
    return jax.shard_map(
        functools.partial(on_device, mesh.shape["row"], mesh.shape["col"]),
        mesh=mesh, in_specs=in_specs, out_specs=out_specs, check_vma=False,
    )
```

```python
import functools
import math

import jax
import jax.numpy as jnp
from jax import lax
from jax.experimental import pallas as pl
from jax.experimental.pallas import tpu as pltpu
from jax.sharding import PartitionSpec as P

ITERS = 3
EPSILON = 0.01
LANES = 128
MESH = pl.DeviceIdType.MESH


def kernel(
    nr, nc, noise, lat,
    out, row_out, col_out,
    noise_all, lat_all, logits, plan, rowb, mt, st, mc, sc, colp,
    row_box, col_box, x_send, x_recv, own, z_low, z_high, num, turned, result, out_box, row_swap, col_swap,
    local_sem, ng_send, ng_recv, lg_send, lg_recv,
    row_send, row_recv, col_send, col_recv,
    xs_sem, xr_sem, up_sem, low_sem, down_sem, high_sem, swap_send, swap_recv, out_send, out_recv,
):
    rows, kn = noise.shape
    cols, kl = lat.shape
    width = kl * nr
    hi = nc // 2
    groups = cols // LANES
    scale = 2.0 / (width * EPSILON)
    row = lax.axis_index("row")
    col = lax.axis_index("col")
    ch, cl = lax.div(col, 2), lax.rem(col, 2)
    rh, rl = lax.div(row, 2), lax.rem(row, 2)
    r, c = 2 * rh + cl, 2 * ch + rl
    h, l = ch, rl
    turn = rl != cl
    half_r = nr // 2

    def along_col(j):
        return {"row": 2 * rh + lax.rem(j, 2), "col": 2 * lax.div(j, 2) + cl}

    def along_row(j):
        return {"row": 2 * lax.div(j, 2) + rl, "col": 2 * ch + lax.rem(j, 2)}

    across = {"row": 2 * rh + 1 - rl, "col": 2 * ch + 1 - cl}

    barrier = pltpu.get_barrier_semaphore()

    def greet(device):
        pl.semaphore_signal(barrier, inc=1, device_id=device, device_id_type=MESH)

    for d in range(1, nc):
        greet(along_col(lax.rem(c + d, nc)))
    for d in range(1, nr):
        greet(along_row(lax.rem(r + d, nr)))
    for d in range(1, half_r):
        greet({"row": 2 * lax.rem(rh + d, half_r) + 1 - rl, "col": col})
    greet(across)
    pl.semaphore_wait(barrier, nc - 1 + nr - 1 + half_r - 1 + 1)

    def noise_slot(j):
        return noise_all.at[lax.div(j, 2), :, pl.ds(pl.multiple_of(lax.rem(j, 2) * kn, kn), kn)]

    def remote(src, dst, send, recv, device):
        return pltpu.make_async_remote_copy(
            src_ref=src, dst_ref=dst, send_sem=send, recv_sem=recv,
            device_id=device, device_id_type=MESH,
        )

    class Gather:
        def __init__(self, along, n, own_ref, slot, send, recv, ah, al):
            self.along, self.half, self.own, self.slot = along, n // 2, own_ref, slot
            self.send, self.recv, self.h, self.l = send, recv, ah, al
            self.me = 2 * ah + al

        def copy(self, kind, j, src):
            target = (self.me + 1 - 2 * self.l, self.me + 2, self.me - 2)[kind]
            return remote(
                src, self.slot(j), self.send.at[kind, lax.div(j, 2)], self.recv.at[j], self.along(target)
            )

        def first(self):
            @pl.when(self.h < self.half - 1)
            def _():
                self.copy(1, self.me, self.own).start()

            @pl.when(self.h > 0)
            def _():
                self.copy(2, self.me, self.own).start()

            self.copy(0, self.me, self.own).start()

        def arrived(self, j):
            self.copy(0, j, self.slot(j)).wait_recv()

        def forward(self, s):
            @pl.when(self.h - s >= 0)
            def _():
                j = self.me - 2 * s
                self.arrived(j)

                @pl.when(self.h < self.half - 1)
                def _():
                    self.copy(1, j, self.slot(j)).start()

                self.copy(0, j, self.slot(j)).start()

            @pl.when(self.h + s < self.half)
            def _():
                j = self.me + 2 * s
                self.arrived(j)

                @pl.when(self.h > 0)
                def _():
                    self.copy(2, j, self.slot(j)).start()

                self.copy(0, j, self.slot(j)).start()

        def other(self, k):
            self.arrived(2 * k + 1 - self.l)

        def finish(self):
            @pl.loop(0, self.half)
            def _(k):
                j = 2 * k + self.l
                self.copy(0, j, self.slot(j)).wait_send()

                @pl.when((k <= self.h) & (self.h < self.half - 1))
                def _():
                    self.copy(1, j, self.slot(j)).wait_send()

                @pl.when((k >= self.h) & (self.h > 0))
                def _():
                    self.copy(2, j, self.slot(j)).wait_send()

    noise_g = Gather(along_col, nc, noise, noise_slot, ng_send, ng_recv, h, l)
    cut = cols * 3 // 8
    lat_span = (pl.ds(0, cut), pl.ds(cut, cols - cut))

    def lat_part(j, p):
        return lat_all.at[j, lat_span[p]]

    def lat_own(p):
        return lat.at[lat_span[p]]

    def lat_copy(kind, j, p, src=None):
        home = {"row": 2 * rh + cl, "col": col}
        side = {"row": 2 * rh + cl, "col": 2 * ch + 1 - cl}
        up = {"row": 2 * (rh + 1) + cl, "col": col}
        down = {"row": 2 * (rh - 1) + cl, "col": col}
        device = (home, side, up, down)[kind]
        return remote(
            lat_part(j, p) if src is None else src, lat_part(j, p),
            lg_send.at[kind, j, p], lg_recv.at[j, p], device,
        )

    def lat_relay(kind, j, p):
        device = (
            None, {"row": row, "col": 2 * ch + 1 - cl},
            {"row": row + 2, "col": col}, {"row": row - 2, "col": col},
        )[kind]
        return remote(lat_part(j, p), lat_part(j, p), lg_send.at[kind, j, p], lg_recv.at[j, p], device)

    def lat_arrived(j, p):
        lat_relay(1, j, p).wait_recv()

    def lat_side(act, p):
        act(lat_copy(1, row, p, lat_own(p)))

    def lat_home(act):
        for p in (1, 0):
            act(lat_copy(0, row, p, lat_own(p)))

    def lat_line(act, p):
        @pl.when(rh < half_r - 1)
        def _():
            act(lat_copy(2, row, p, lat_own(p)))

        @pl.when(rh > 0)
        def _():
            act(lat_copy(3, row, p, lat_own(p)))

    def start(copy):
        copy.start()

    def wait_send(copy):
        copy.wait_send()

    def lat_pass(act, wait):
        @pl.when(turn)
        def _():
            for q in range(2):
                j = 2 * rh + q
                wait(j, 1)

                @pl.when(rh < half_r - 1)
                def _():
                    act(lat_relay(2, j, 1))

                @pl.when(rh > 0)
                def _():
                    act(lat_relay(3, j, 1))

        for s in range(1, half_r):
            for sign, kind in ((-1, 2), (1, 3)):
                k = rh + sign * s
                onward = (rh < half_r - 1) if sign < 0 else (rh > 0)
                valid = (k >= 0) if sign < 0 else (k < half_r)

                @pl.when(valid)
                def _():
                    for q in range(2):
                        j = 2 * k + q
                        if half_r > 2:
                            @pl.when(turn)
                            def _():
                                wait(j, 1)

                                @pl.when(onward)
                                def _():
                                    act(lat_relay(kind, j, 1))

                        @pl.when(jnp.logical_not(turn))
                        def _():
                            wait(j, 0)
                            act(lat_relay(1, j, 0))

                            @pl.when(onward)
                            def _():
                                act(lat_relay(kind, j, 0))
                                wait(j, 1)
                                act(lat_relay(kind, j, 1))

    def lat_ready(k):
        kh, kq = lax.div(k, 2), lax.rem(k, 2)
        near = kh == rh
        onward = ((kh < rh) & (rh < half_r - 1)) | ((kh > rh) & (rh > 0))

        @pl.when(turn)
        def _():
            lat_arrived(k, 0)
            if half_r == 2:
                @pl.when(jnp.logical_not(near))
                def _():
                    lat_arrived(k, 1)

        @pl.when(jnp.logical_not(turn) & near & (kq != rl))
        def _():
            lat_arrived(k, 0)
            lat_arrived(k, 1)

        @pl.when(jnp.logical_not(turn) & jnp.logical_not(near) & jnp.logical_not(onward))
        def _():
            lat_arrived(k, 1)

    noise_swap = remote(noise, turned, swap_send.at[0], swap_recv.at[0], across)

    @pl.when(turn)
    def _():
        noise_swap.start()

    @pl.when(jnp.logical_not(turn))
    def _():
        noise_g.first()

    lat_line(start, 0)
    keep_noise = pltpu.make_async_copy(noise, noise_slot(c), local_sem.at[0])
    keep_turned = pltpu.make_async_copy(turned, noise_slot(c), local_sem.at[0])
    keep_lat = pltpu.make_async_copy(lat, lat_all.at[row], local_sem.at[1])

    @pl.when(jnp.logical_not(turn))
    def _():
        keep_noise.start()
        keep_lat.start()

    @pl.when(turn)
    def _():
        noise_swap.wait_recv()
        noise_g.own = turned
        noise_g.first()
        lat_side(start, 1)
        keep_turned.start()
        lat_home(start)

    colp[...] = jnp.zeros_like(colp)

    tile_n = min(256, cols)

    def block(k, add):
        @pl.loop(0, cols // tile_n)
        def _(t):
            span = pl.ds(pl.multiple_of(t * tile_n, tile_n), tile_n)
            part = lax.dot_general(
                noise_all[k], lat_all[k, span, :], (((1,), (1,)), ((), ())),
                preferred_element_type=jnp.float32,
            ) * scale
            if add:
                logits[:, span] += part
            else:
                logits[:, span] = part

    def noise_ready(k):
        noise_g.other(k)

    noise_g.forward(1)

    @pl.when(jnp.logical_not(turn))
    def _():
        lat_side(start, 1)

    lat_line(wait_send, 0)
    lat_line(start, 1)
    lat_pass(start, lat_arrived)
    lat_side(start, 0)
    for s in range(2, hi - 1):
        noise_g.forward(s)

    @pl.when(jnp.logical_not(turn))
    def _():
        keep_noise.wait()
        keep_lat.wait()

    @pl.when(turn)
    def _():
        keep_turned.wait()

    near = jnp.minimum(jnp.maximum(h, 2 * rh), 2 * rh + 1)
    noise_ready(near)
    lat_ready(near)
    block(near, False)
    if hi > 2:
        noise_g.forward(hi - 1)

    @pl.loop(1, hi)
    def _(i):
        k = jnp.where(i == 1, 4 * rh + 1 - near, lax.rem(2 * rh + i, hi))
        noise_ready(k)
        lat_ready(k)
        block(k, True)

    def exchange(along, n, me, box, send, recv):
        for d in range(1, n):
            remote(box.at[me], box.at[me], send.at[d], recv.at[me], along(lax.rem(me + d, n))).start()
        for d in range(1, n):
            j = lax.rem(me + n - d, n)
            remote(box.at[j], box.at[j], send.at[d], recv.at[j], along(j)).wait_recv()

    def sent(along, n, me, box, send, recv):
        for d in range(1, n):
            remote(box.at[me], box.at[me], send.at[d], recv.at[me], along(lax.rem(me + d, n))).wait_send()

    def merged(n, box):
        high = functools.reduce(jnp.maximum, [box[j, 0:1, :] for j in range(n)])
        total = functools.reduce(
            jnp.add, [box[j, 1:2, :] * jnp.exp(box[j, 0:1, :] - high) for j in range(n)]
        )
        return high + jnp.log(total)

    def lane(g):
        return pl.ds(g * LANES, LANES)

    row_tile = 32
    col_tile = 64

    for step in range(ITERS):
        @pl.loop(0, rows // row_tile, unroll=2)
        def _(t):
            span = pl.ds(pl.multiple_of(t * row_tile, row_tile), row_tile)
            v = [logits[span, lane(g)] + colp[:, lane(g)] for g in range(groups)]
            m = functools.reduce(jnp.maximum, v)
            mt[span, :] = m
            st[span, :] = functools.reduce(jnp.add, [jnp.exp(x - m) for x in v])

        m = mt[...].T
        high = jnp.max(m, axis=0, keepdims=True)
        box = row_box.at[step]
        mine_box = box.at[c]
        mine_box[0:1, :] = high
        mine_box[1:2, :] = jnp.sum(st[...].T * jnp.exp(m - high), axis=0, keepdims=True)
        exchange(along_col, nc, c, box, row_send.at[step], row_recv.at[step])
        rowp = -math.log(rows * nr) - merged(nc, box)
        row_swap[0] = rowp
        rowb[...] = jnp.broadcast_to(rowp, (LANES, rows)).T

        @pl.loop(0, rows // col_tile)
        def _(t):
            span = pl.ds(pl.multiple_of(t * col_tile, col_tile), col_tile)
            small = pl.ds(pl.multiple_of(t * 8, 8), 8)
            shift = rowb[span, :]
            for g in range(groups):
                v = (logits[span, lane(g)] + shift).reshape(col_tile // 8, 8, LANES)
                m = jnp.max(v, axis=0)
                mc[small, lane(g)] = m
                sc[small, lane(g)] = jnp.sum(jnp.exp(v - m[None]), axis=0)

        m = mc[...]
        high = jnp.max(m, axis=0, keepdims=True)
        box = col_box.at[step]
        mine_box = box.at[r]
        mine_box[0:1, :] = high
        mine_box[1:2, :] = jnp.sum(sc[...] * jnp.exp(m - high), axis=0, keepdims=True)
        exchange(along_row, nr, r, box, col_send.at[step], col_recv.at[step])
        colp[...] = -math.log(cols * nc) - merged(nr, box)
    row_pair = remote(row_swap.at[0], row_swap.at[1], swap_send.at[1], swap_recv.at[1], across)
    col_pair = remote(colp, col_swap, swap_send.at[2], swap_recv.at[2], across)

    @pl.when(turn)
    def _():
        row_pair.start()
        col_pair.start()

    @pl.when(jnp.logical_not(turn))
    def _():
        row_out[...] = row_swap[0]
        col_out[...] = colp[...]


    @pl.loop(0, rows // row_tile, unroll=2)
    def _(t):
        span = pl.ds(pl.multiple_of(t * row_tile, row_tile), row_tile)
        shift = rowb[span, :]
        total = jnp.zeros((row_tile, LANES), jnp.float32)
        for g in range(groups):
            p = jnp.exp(logits[span, lane(g)] + shift + colp[:, lane(g)]).astype(jnp.bfloat16)
            plan[span, lane(g)] = p
            total += p.astype(jnp.float32)
        mt[span, :] = total

    tile_k = min(256, kn)

    parts = 4
    part = rows // parts
    add_tile = min(128, part)

    def rows_of(p):
        return pl.ds(pl.multiple_of(p * part, part), part)

    def share(k, side, p, dst):
        @pl.loop(0, kn // tile_k)
        def _(t):
            off = pl.multiple_of(t * tile_k, tile_k)
            src = pl.multiple_of(side * kn + t * tile_k, tile_k)
            dst[k, rows_of(p), pl.ds(off, tile_k)] = jnp.dot(
                plan[rows_of(p), :], lat_all[k, :, pl.ds(src, tile_k)], preferred_element_type=jnp.float32
            ).astype(jnp.bfloat16)

    def piece(ref, k, p):
        return ref.at[k, rows_of(p)]

    def x_copy(k, p):
        return remote(
            piece(x_send, k, p), piece(x_recv, k, p), xs_sem.at[k, p], xr_sem.at[k, p],
            along_col(c + 1 - 2 * l),
        )

    def up_copy(k, p):
        return remote(
            piece(own, k, p), piece(z_low, k, p), up_sem.at[k, p], low_sem.at[k, p], along_col(c + 2)
        )

    def down_copy(k, p):
        return remote(
            piece(own, k, p), piece(z_high, k, p), down_sem.at[k, p], high_sem.at[k, p], along_col(c - 2)
        )

    def farthest_first(body):
        @pl.loop(0, 2 * hi - 1)
        def _(p):
            s = hi - 1 - lax.div(p, 2)
            k = h + s * (1 - 2 * lax.rem(p, 2))

            @pl.when((k >= 0) & (k < hi))
            def _():
                body(k)

    f32, bf16 = jnp.float32, jnp.bfloat16

    def tiles(p, body):
        @pl.loop(0, part // add_tile)
        def _(t):
            body(pl.ds(pl.multiple_of(p * part + t * add_tile, add_tile), add_tile))

    def add(k, p, third):
        def body(span):
            total = own[k, span, :].astype(f32) + third[k, span, :].astype(f32)
            own[k, span, :] = total.astype(bf16)
        tiles(p, body)

    def work(k):
        @pl.loop(0, parts)
        def _(p):
            share(k, 1 - l, p, x_send)
            x_copy(k, p).start()

        @pl.loop(0, parts)
        def _(p):
            share(k, l, p, own)
            x_copy(k, p).wait_recv()
            add(k, p, x_recv)

            @pl.when((k > h) & (h == 0))
            def _():
                up_copy(k, p).start()

            @pl.when((k < h) & (h == hi - 1))
            def _():
                down_copy(k, p).start()

    farthest_first(work)

    mine_box = row_box.at[ITERS, c]
    mine_box[0:1, :] = jnp.sum(mt[...].T, axis=0, keepdims=True)
    mine_box[1:2, :] = jnp.zeros((1, rows), f32)
    exchange(along_col, nc, c, row_box.at[ITERS], row_send.at[ITERS], row_recv.at[ITERS])
    mass = functools.reduce(jnp.add, [row_box[ITERS, j, 0:1, :] for j in range(nc)])
    rowb[...] = jnp.broadcast_to(1.0 / mass, (LANES, rows)).T

    def relay(k):
        @pl.loop(0, parts)
        def _(p):
            @pl.when((k > h) & (h > 0))
            def _():
                up_copy(k, p).wait_recv()
                add(k, p, z_low)
                up_copy(k, p).start()

            @pl.when((k < h) & (h < hi - 1))
            def _():
                down_copy(k, p).wait_recv()
                add(k, p, z_high)
                down_copy(k, p).start()

    farthest_first(relay)

    def out_copy(p):
        span = rows_of(p)
        return remote(result.at[span], out_box.at[span], out_send.at[p], out_recv.at[p], across)

    @pl.loop(0, parts)
    def _(p):
        def start_sum(span):
            num[span, :] = own[h, span, :].astype(f32)

        tiles(p, start_sum)

        def add_low(span):
            num[span, :] += z_low[h, span, :].astype(f32)

        def add_high(span):
            num[span, :] += z_high[h, span, :].astype(f32)

        @pl.when(h > 0)
        def _():
            up_copy(h, p).wait_recv()
            tiles(p, add_low)

        @pl.when(h < hi - 1)
        def _():
            down_copy(h, p).wait_recv()
            tiles(p, add_high)

        def divide(ref):
            def body(span):
                inverse = rowb[span, :]
                for g in range(kn // LANES):
                    ref[span, lane(g)] = (num[span, lane(g)] * inverse).astype(bf16)
            tiles(p, body)

        @pl.when(turn)
        def _():
            divide(result)
            out_copy(p).start()

        @pl.when(jnp.logical_not(turn))
        def _():
            divide(out)

    @pl.when(turn)
    def _():
        row_pair.wait()
        col_pair.wait()
        row_out[...] = row_swap[1]
        col_out[...] = col_swap[...]
        for p in range(parts):
            out_copy(p).wait_recv()

            def body(span):
                out[span, :] = out_box[span, :]
            tiles(p, body)
        for p in range(parts):
            out_copy(p).wait_send()
        noise_swap.wait_send()

    noise_g.finish()
    lat_side(wait_send, 0)
    lat_side(wait_send, 1)
    lat_line(wait_send, 1)

    @pl.when(turn)
    def _():
        lat_home(wait_send)

    lat_pass(wait_send, lambda j, p: None)
    for step in range(ITERS + 1):
        sent(along_col, nc, c, row_box.at[step], row_send.at[step], row_recv.at[step])
    for step in range(ITERS):
        sent(along_row, nr, r, col_box.at[step], col_send.at[step], col_recv.at[step])

    @pl.loop(0, hi)
    def _(k):
        @pl.loop(0, parts)
        def _(p):
            x_copy(k, p).wait_send()

            @pl.when(k > h)
            def _():
                up_copy(k, p).wait_send()

            @pl.when(k < h)
            def _():
                down_copy(k, p).wait_send()


def on_device(nr, nc, noise, latents):
    rows, kn = noise.shape
    cols, kl = latents.shape
    hi = nc // 2
    bf16, f32 = jnp.bfloat16, jnp.float32
    vmem, dma = pltpu.VMEM, pltpu.SemaphoreType.DMA
    transported, row_potential, col_potential = pl.pallas_call(
        functools.partial(kernel, nr, nc),
        out_shape=(
            jax.ShapeDtypeStruct((rows, kn), bf16),
            jax.ShapeDtypeStruct((1, rows), f32),
            jax.ShapeDtypeStruct((1, cols), f32),
        ),
        in_specs=[pl.BlockSpec(memory_space=pl.ANY)] * 2,
        out_specs=[pl.BlockSpec(memory_space=pltpu.VMEM)] * 3,
        scratch_shapes=[
            vmem((hi, rows, 2 * kn), bf16),
            vmem((nr, cols, kl), bf16),
            vmem((rows, cols), f32),
            vmem((rows, cols), bf16),
            vmem((rows, LANES), f32),
            vmem((rows, LANES), f32),
            vmem((rows, LANES), f32),
            vmem((rows // 8, cols), f32),
            vmem((rows // 8, cols), f32),
            vmem((1, cols), f32),
            vmem((ITERS + 1, nc, 2, rows), f32),
            vmem((ITERS, nr, 2, cols), f32),
            vmem((hi, rows, kn), bf16),
            vmem((hi, rows, kn), bf16),
            vmem((hi, rows, kn), bf16),
            vmem((hi, rows, kn), bf16),
            vmem((hi, rows, kn), bf16),
            vmem((rows, kn), f32),
            vmem((rows, kn), bf16),
            vmem((rows, kn), bf16),
            vmem((rows, kn), bf16),
            vmem((2, 1, rows), f32),
            vmem((1, cols), f32),
            dma((2,)),
            dma((3, hi)), dma((nc,)),
            dma((4, nr, 2)), dma((nr, 2)),
            dma((ITERS + 1, nc)), dma((ITERS + 1, nc)),
            dma((ITERS, nr)), dma((ITERS, nr)),
            dma((hi, 4)), dma((hi, 4)), dma((hi, 4)), dma((hi, 4)), dma((hi, 4)), dma((hi, 4)),
            dma((3,)), dma((3,)), dma((4,)), dma((4,)),
        ],
        compiler_params=pltpu.CompilerParams(
            collective_id=0, has_side_effects=True, vmem_limit_bytes=58 * 2**20
        ),
        cost_estimate=pl.CostEstimate(
            flops=4 * rows * cols * kl * nr, bytes_accessed=8 * 2**20, transcendentals=7 * rows * cols
        ),
    )(noise, latents)
    return transported, row_potential.reshape(rows), col_potential.reshape(cols)


def solution(mesh):
    in_specs = (P("row", "col"), P("col", "row"))
    out_specs = (P("row", "col"), P("row"), P("col"))
    return jax.shard_map(
        functools.partial(on_device, mesh.shape["row"], mesh.shape["col"]),
        mesh=mesh, in_specs=in_specs, out_specs=out_specs, check_vma=False,
    )
```

```python
import functools
import math

import jax
import jax.numpy as jnp
from jax import lax
from jax.experimental import pallas as pl
from jax.experimental.pallas import tpu as pltpu
from jax.sharding import PartitionSpec as P

ITERS = 3
EPSILON = 0.01
LANES = 128
MESH = pl.DeviceIdType.MESH


def kernel(
    nr, nc, noise, lat,
    out, row_out, col_out,
    noise_all, lat_all, logits, plan, rowb, mt, st, mc, sc, colp,
    row_box, col_box, x_send, x_recv, own, z_low, z_high, num, turned, result, out_box, row_swap, col_swap,
    local_sem, ng_send, ng_recv, lg_send, lg_recv,
    row_send, row_recv, col_send, col_recv,
    xs_sem, xr_sem, up_sem, low_sem, down_sem, high_sem, swap_send, swap_recv, out_send, out_recv,
):
    rows, kn = noise.shape
    cols, kl = lat.shape
    width = kl * nr
    hi = nc // 2
    groups = cols // LANES
    scale = 2.0 / (width * EPSILON)
    row = lax.axis_index("row")
    col = lax.axis_index("col")
    ch, cl = lax.div(col, 2), lax.rem(col, 2)
    rh, rl = lax.div(row, 2), lax.rem(row, 2)
    r, c = 2 * rh + cl, 2 * ch + rl
    h, l = ch, rl
    turn = rl != cl
    half_r = nr // 2

    def along_col(j):
        return {"row": 2 * rh + lax.rem(j, 2), "col": 2 * lax.div(j, 2) + cl}

    def along_row(j):
        return {"row": 2 * lax.div(j, 2) + rl, "col": 2 * ch + lax.rem(j, 2)}

    across = {"row": 2 * rh + 1 - rl, "col": 2 * ch + 1 - cl}

    barrier = pltpu.get_barrier_semaphore()

    def greet(device):
        pl.semaphore_signal(barrier, inc=1, device_id=device, device_id_type=MESH)

    for d in range(1, nc):
        greet(along_col(lax.rem(c + d, nc)))
    for d in range(1, nr):
        greet(along_row(lax.rem(r + d, nr)))
    for d in range(1, half_r):
        greet({"row": 2 * lax.rem(rh + d, half_r) + 1 - rl, "col": col})
    greet(across)
    pl.semaphore_wait(barrier, nc - 1 + nr - 1 + half_r - 1 + 1)

    def noise_slot(j):
        return noise_all.at[lax.div(j, 2), :, pl.ds(pl.multiple_of(lax.rem(j, 2) * kn, kn), kn)]

    def remote(src, dst, send, recv, device):
        return pltpu.make_async_remote_copy(
            src_ref=src, dst_ref=dst, send_sem=send, recv_sem=recv,
            device_id=device, device_id_type=MESH,
        )

    class Gather:
        def __init__(self, along, n, own_ref, slot, send, recv, ah, al):
            self.along, self.half, self.own, self.slot = along, n // 2, own_ref, slot
            self.send, self.recv, self.h, self.l = send, recv, ah, al
            self.me = 2 * ah + al

        def copy(self, kind, j, src):
            target = (self.me + 1 - 2 * self.l, self.me + 2, self.me - 2)[kind]
            return remote(
                src, self.slot(j), self.send.at[kind, lax.div(j, 2)], self.recv.at[j], self.along(target)
            )

        def first(self):
            @pl.when(self.h < self.half - 1)
            def _():
                self.copy(1, self.me, self.own).start()

            @pl.when(self.h > 0)
            def _():
                self.copy(2, self.me, self.own).start()

            self.copy(0, self.me, self.own).start()

        def arrived(self, j):
            self.copy(0, j, self.slot(j)).wait_recv()

        def forward(self, s):
            @pl.when(self.h - s >= 0)
            def _():
                j = self.me - 2 * s
                self.arrived(j)

                @pl.when(self.h < self.half - 1)
                def _():
                    self.copy(1, j, self.slot(j)).start()

                self.copy(0, j, self.slot(j)).start()

            @pl.when(self.h + s < self.half)
            def _():
                j = self.me + 2 * s
                self.arrived(j)

                @pl.when(self.h > 0)
                def _():
                    self.copy(2, j, self.slot(j)).start()

                self.copy(0, j, self.slot(j)).start()

        def other(self, k):
            self.arrived(2 * k + 1 - self.l)

        def finish(self):
            @pl.loop(0, self.half)
            def _(k):
                j = 2 * k + self.l
                self.copy(0, j, self.slot(j)).wait_send()

                @pl.when((k <= self.h) & (self.h < self.half - 1))
                def _():
                    self.copy(1, j, self.slot(j)).wait_send()

                @pl.when((k >= self.h) & (self.h > 0))
                def _():
                    self.copy(2, j, self.slot(j)).wait_send()

    noise_g = Gather(along_col, nc, noise, noise_slot, ng_send, ng_recv, h, l)
    cut = cols * 3 // 8
    lat_span = (pl.ds(0, cut), pl.ds(cut, cols - cut))

    def lat_part(j, p):
        return lat_all.at[j, lat_span[p]]

    def lat_own(p):
        return lat.at[lat_span[p]]

    def lat_copy(kind, j, p, src=None):
        home = {"row": 2 * rh + cl, "col": col}
        side = {"row": 2 * rh + cl, "col": 2 * ch + 1 - cl}
        up = {"row": 2 * (rh + 1) + cl, "col": col}
        down = {"row": 2 * (rh - 1) + cl, "col": col}
        device = (home, side, up, down)[kind]
        return remote(
            lat_part(j, p) if src is None else src, lat_part(j, p),
            lg_send.at[kind, j, p], lg_recv.at[j, p], device,
        )

    def lat_relay(kind, j, p):
        device = (
            None, {"row": row, "col": 2 * ch + 1 - cl},
            {"row": row + 2, "col": col}, {"row": row - 2, "col": col},
        )[kind]
        return remote(lat_part(j, p), lat_part(j, p), lg_send.at[kind, j, p], lg_recv.at[j, p], device)

    def lat_arrived(j, p):
        lat_relay(1, j, p).wait_recv()

    def lat_side(act):
        for p in (1, 0):
            act(lat_copy(1, row, p, lat_own(p)))

    def lat_home(act):
        for p in (1, 0):
            act(lat_copy(0, row, p, lat_own(p)))

    def lat_line(act, p):
        @pl.when(rh < half_r - 1)
        def _():
            act(lat_copy(2, row, p, lat_own(p)))

        @pl.when(rh > 0)
        def _():
            act(lat_copy(3, row, p, lat_own(p)))

    def start(copy):
        copy.start()

    def wait_send(copy):
        copy.wait_send()

    def lat_pass(act, wait):
        @pl.when(turn)
        def _():
            for q in range(2):
                j = 2 * rh + q
                wait(j, 1)

                @pl.when(rh < half_r - 1)
                def _():
                    act(lat_relay(2, j, 1))

                @pl.when(rh > 0)
                def _():
                    act(lat_relay(3, j, 1))

        for s in range(1, half_r):
            for sign, kind in ((-1, 2), (1, 3)):
                k = rh + sign * s
                onward = (rh < half_r - 1) if sign < 0 else (rh > 0)
                valid = (k >= 0) if sign < 0 else (k < half_r)

                @pl.when(valid)
                def _():
                    for q in range(2):
                        j = 2 * k + q
                        if half_r > 2:
                            @pl.when(turn)
                            def _():
                                wait(j, 1)

                                @pl.when(onward)
                                def _():
                                    act(lat_relay(kind, j, 1))

                        @pl.when(jnp.logical_not(turn))
                        def _():
                            wait(j, 0)
                            act(lat_relay(1, j, 0))

                            @pl.when(onward)
                            def _():
                                act(lat_relay(kind, j, 0))
                                wait(j, 1)
                                act(lat_relay(kind, j, 1))

    def lat_ready(k):
        kh, kq = lax.div(k, 2), lax.rem(k, 2)
        near = kh == rh
        onward = ((kh < rh) & (rh < half_r - 1)) | ((kh > rh) & (rh > 0))

        @pl.when(turn)
        def _():
            lat_arrived(k, 0)
            if half_r == 2:
                @pl.when(jnp.logical_not(near))
                def _():
                    lat_arrived(k, 1)

        @pl.when(jnp.logical_not(turn) & near & (kq != rl))
        def _():
            lat_arrived(k, 0)
            lat_arrived(k, 1)

        @pl.when(jnp.logical_not(turn) & jnp.logical_not(near) & jnp.logical_not(onward))
        def _():
            lat_arrived(k, 1)

    noise_swap = remote(noise, turned, swap_send.at[0], swap_recv.at[0], across)

    @pl.when(turn)
    def _():
        noise_swap.start()

    @pl.when(jnp.logical_not(turn))
    def _():
        noise_g.first()

    lat_side(start)
    lat_line(start, 0)
    lat_line(start, 1)

    @pl.when(turn)
    def _():
        lat_home(start)

    keep_noise = pltpu.make_async_copy(noise, noise_slot(c), local_sem.at[0])
    keep_turned = pltpu.make_async_copy(turned, noise_slot(c), local_sem.at[0])
    keep_lat = pltpu.make_async_copy(lat, lat_all.at[row], local_sem.at[1])

    @pl.when(jnp.logical_not(turn))
    def _():
        keep_noise.start()
        keep_lat.start()

    @pl.when(turn)
    def _():
        noise_swap.wait_recv()
        noise_g.own = turned
        noise_g.first()
        keep_turned.start()

    colp[...] = jnp.zeros_like(colp)

    tile_n = min(256, cols)

    def block(k, add):
        @pl.loop(0, cols // tile_n)
        def _(t):
            span = pl.ds(pl.multiple_of(t * tile_n, tile_n), tile_n)
            part = lax.dot_general(
                noise_all[k], lat_all[k, span, :], (((1,), (1,)), ((), ())),
                preferred_element_type=jnp.float32,
            ) * scale
            if add:
                logits[:, span] += part
            else:
                logits[:, span] = part

    def noise_ready(k):
        noise_g.other(k)

    noise_g.forward(1)

    lat_pass(start, lat_arrived)
    for s in range(2, hi - 1):
        noise_g.forward(s)

    @pl.when(jnp.logical_not(turn))
    def _():
        keep_noise.wait()
        keep_lat.wait()

    @pl.when(turn)
    def _():
        keep_turned.wait()

    near = jnp.minimum(jnp.maximum(h, 2 * rh), 2 * rh + 1)
    noise_ready(near)
    lat_ready(near)
    block(near, False)
    if hi > 2:
        noise_g.forward(hi - 1)

    @pl.loop(1, hi)
    def _(i):
        k = jnp.where(i == 1, 4 * rh + 1 - near, lax.rem(2 * rh + i, hi))
        noise_ready(k)
        lat_ready(k)
        block(k, True)

    def exchange(along, n, me, box, send, recv):
        for d in range(1, n):
            remote(box.at[me], box.at[me], send.at[d], recv.at[me], along(lax.rem(me + d, n))).start()
        for d in range(1, n):
            j = lax.rem(me + n - d, n)
            remote(box.at[j], box.at[j], send.at[d], recv.at[j], along(j)).wait_recv()

    def sent(along, n, me, box, send, recv):
        for d in range(1, n):
            remote(box.at[me], box.at[me], send.at[d], recv.at[me], along(lax.rem(me + d, n))).wait_send()

    def merged(n, box):
        high = functools.reduce(jnp.maximum, [box[j, 0:1, :] for j in range(n)])
        total = functools.reduce(
            jnp.add, [box[j, 1:2, :] * jnp.exp(box[j, 0:1, :] - high) for j in range(n)]
        )
        return high + jnp.log(total)

    def lane(g):
        return pl.ds(g * LANES, LANES)

    row_tile = 32
    col_tile = 64

    for step in range(ITERS):
        @pl.loop(0, rows // row_tile, unroll=2)
        def _(t):
            span = pl.ds(pl.multiple_of(t * row_tile, row_tile), row_tile)
            v = [logits[span, lane(g)] + colp[:, lane(g)] for g in range(groups)]
            m = functools.reduce(jnp.maximum, v)
            mt[span, :] = m
            st[span, :] = functools.reduce(jnp.add, [jnp.exp(x - m) for x in v])

        m = mt[...].T
        high = jnp.max(m, axis=0, keepdims=True)
        box = row_box.at[step]
        mine_box = box.at[c]
        mine_box[0:1, :] = high
        mine_box[1:2, :] = jnp.sum(st[...].T * jnp.exp(m - high), axis=0, keepdims=True)
        exchange(along_col, nc, c, box, row_send.at[step], row_recv.at[step])
        rowp = -math.log(rows * nr) - merged(nc, box)
        row_swap[0] = rowp
        rowb[...] = jnp.broadcast_to(rowp, (LANES, rows)).T

        @pl.loop(0, rows // col_tile)
        def _(t):
            span = pl.ds(pl.multiple_of(t * col_tile, col_tile), col_tile)
            small = pl.ds(pl.multiple_of(t * 8, 8), 8)
            shift = rowb[span, :]
            for g in range(groups):
                v = (logits[span, lane(g)] + shift).reshape(col_tile // 8, 8, LANES)
                m = jnp.max(v, axis=0)
                mc[small, lane(g)] = m
                sc[small, lane(g)] = jnp.sum(jnp.exp(v - m[None]), axis=0)

        m = mc[...]
        high = jnp.max(m, axis=0, keepdims=True)
        box = col_box.at[step]
        mine_box = box.at[r]
        mine_box[0:1, :] = high
        mine_box[1:2, :] = jnp.sum(sc[...] * jnp.exp(m - high), axis=0, keepdims=True)
        exchange(along_row, nr, r, box, col_send.at[step], col_recv.at[step])
        colp[...] = -math.log(cols * nc) - merged(nr, box)
    row_pair = remote(row_swap.at[0], row_swap.at[1], swap_send.at[1], swap_recv.at[1], across)
    col_pair = remote(colp, col_swap, swap_send.at[2], swap_recv.at[2], across)

    @pl.when(turn)
    def _():
        row_pair.start()
        col_pair.start()

    @pl.when(jnp.logical_not(turn))
    def _():
        row_out[...] = row_swap[0]
        col_out[...] = colp[...]


    @pl.loop(0, rows // row_tile, unroll=2)
    def _(t):
        span = pl.ds(pl.multiple_of(t * row_tile, row_tile), row_tile)
        shift = rowb[span, :]
        total = jnp.zeros((row_tile, LANES), jnp.float32)
        for g in range(groups):
            p = jnp.exp(logits[span, lane(g)] + shift + colp[:, lane(g)]).astype(jnp.bfloat16)
            plan[span, lane(g)] = p
            total += p.astype(jnp.float32)
        mt[span, :] = total

    tile_k = min(256, kn)

    parts = 4
    part = rows // parts
    add_tile = min(128, part)

    def rows_of(p):
        return pl.ds(pl.multiple_of(p * part, part), part)

    def share(k, side, p, dst):
        @pl.loop(0, kn // tile_k)
        def _(t):
            off = pl.multiple_of(t * tile_k, tile_k)
            src = pl.multiple_of(side * kn + t * tile_k, tile_k)
            dst[k, rows_of(p), pl.ds(off, tile_k)] = jnp.dot(
                plan[rows_of(p), :], lat_all[k, :, pl.ds(src, tile_k)], preferred_element_type=jnp.float32
            ).astype(jnp.bfloat16)

    def piece(ref, k, p):
        return ref.at[k, rows_of(p)]

    def x_copy(k, p):
        return remote(
            piece(x_send, k, p), piece(x_recv, k, p), xs_sem.at[k, p], xr_sem.at[k, p],
            along_col(c + 1 - 2 * l),
        )

    def up_copy(k, p):
        return remote(
            piece(own, k, p), piece(z_low, k, p), up_sem.at[k, p], low_sem.at[k, p], along_col(c + 2)
        )

    def down_copy(k, p):
        return remote(
            piece(own, k, p), piece(z_high, k, p), down_sem.at[k, p], high_sem.at[k, p], along_col(c - 2)
        )

    def farthest_first(body):
        @pl.loop(0, 2 * hi - 1)
        def _(p):
            s = hi - 1 - lax.div(p, 2)
            k = h + s * (1 - 2 * lax.rem(p, 2))

            @pl.when((k >= 0) & (k < hi))
            def _():
                body(k)

    f32, bf16 = jnp.float32, jnp.bfloat16

    def tiles(p, body):
        @pl.loop(0, part // add_tile)
        def _(t):
            body(pl.ds(pl.multiple_of(p * part + t * add_tile, add_tile), add_tile))

    def add(k, p, third):
        def body(span):
            total = own[k, span, :].astype(f32) + third[k, span, :].astype(f32)
            own[k, span, :] = total.astype(bf16)
        tiles(p, body)

    def work(k):
        @pl.loop(0, parts)
        def _(p):
            share(k, 1 - l, p, x_send)
            x_copy(k, p).start()

        @pl.loop(0, parts)
        def _(p):
            share(k, l, p, own)
            x_copy(k, p).wait_recv()
            add(k, p, x_recv)

            @pl.when((k > h) & (h == 0))
            def _():
                up_copy(k, p).start()

            @pl.when((k < h) & (h == hi - 1))
            def _():
                down_copy(k, p).start()

    farthest_first(work)

    mine_box = row_box.at[ITERS, c]
    mine_box[0:1, :] = jnp.sum(mt[...].T, axis=0, keepdims=True)
    mine_box[1:2, :] = jnp.zeros((1, rows), f32)
    exchange(along_col, nc, c, row_box.at[ITERS], row_send.at[ITERS], row_recv.at[ITERS])
    mass = functools.reduce(jnp.add, [row_box[ITERS, j, 0:1, :] for j in range(nc)])
    rowb[...] = jnp.broadcast_to(1.0 / mass, (LANES, rows)).T

    def relay(k):
        @pl.loop(0, parts)
        def _(p):
            @pl.when((k > h) & (h > 0))
            def _():
                up_copy(k, p).wait_recv()
                add(k, p, z_low)
                up_copy(k, p).start()

            @pl.when((k < h) & (h < hi - 1))
            def _():
                down_copy(k, p).wait_recv()
                add(k, p, z_high)
                down_copy(k, p).start()

    farthest_first(relay)

    def out_copy(p):
        span = rows_of(p)
        return remote(result.at[span], out_box.at[span], out_send.at[p], out_recv.at[p], across)

    @pl.loop(0, parts)
    def _(p):
        def start_sum(span):
            num[span, :] = own[h, span, :].astype(f32)

        tiles(p, start_sum)

        def add_low(span):
            num[span, :] += z_low[h, span, :].astype(f32)

        def add_high(span):
            num[span, :] += z_high[h, span, :].astype(f32)

        @pl.when(h > 0)
        def _():
            up_copy(h, p).wait_recv()
            tiles(p, add_low)

        @pl.when(h < hi - 1)
        def _():
            down_copy(h, p).wait_recv()
            tiles(p, add_high)

        def divide(ref):
            def body(span):
                inverse = rowb[span, :]
                for g in range(kn // LANES):
                    ref[span, lane(g)] = (num[span, lane(g)] * inverse).astype(bf16)
            tiles(p, body)

        @pl.when(turn)
        def _():
            divide(result)
            out_copy(p).start()

        @pl.when(jnp.logical_not(turn))
        def _():
            divide(out)

    @pl.when(turn)
    def _():
        row_pair.wait()
        col_pair.wait()
        row_out[...] = row_swap[1]
        col_out[...] = col_swap[...]
        for p in range(parts):
            out_copy(p).wait_recv()

            def body(span):
                out[span, :] = out_box[span, :]
            tiles(p, body)
        for p in range(parts):
            out_copy(p).wait_send()
        noise_swap.wait_send()

    noise_g.finish()
    lat_side(wait_send)
    lat_line(wait_send, 0)
    lat_line(wait_send, 1)

    @pl.when(turn)
    def _():
        lat_home(wait_send)

    lat_pass(wait_send, lambda j, p: None)
    for step in range(ITERS + 1):
        sent(along_col, nc, c, row_box.at[step], row_send.at[step], row_recv.at[step])
    for step in range(ITERS):
        sent(along_row, nr, r, col_box.at[step], col_send.at[step], col_recv.at[step])

    @pl.loop(0, hi)
    def _(k):
        @pl.loop(0, parts)
        def _(p):
            x_copy(k, p).wait_send()

            @pl.when(k > h)
            def _():
                up_copy(k, p).wait_send()

            @pl.when(k < h)
            def _():
                down_copy(k, p).wait_send()


def on_device(nr, nc, noise, latents):
    rows, kn = noise.shape
    cols, kl = latents.shape
    hi = nc // 2
    bf16, f32 = jnp.bfloat16, jnp.float32
    vmem, dma = pltpu.VMEM, pltpu.SemaphoreType.DMA
    transported, row_potential, col_potential = pl.pallas_call(
        functools.partial(kernel, nr, nc),
        out_shape=(
            jax.ShapeDtypeStruct((rows, kn), bf16),
            jax.ShapeDtypeStruct((1, rows), f32),
            jax.ShapeDtypeStruct((1, cols), f32),
        ),
        in_specs=[pl.BlockSpec(memory_space=pl.ANY)] * 2,
        out_specs=[pl.BlockSpec(memory_space=pltpu.VMEM)] * 3,
        scratch_shapes=[
            vmem((hi, rows, 2 * kn), bf16),
            vmem((nr, cols, kl), bf16),
            vmem((rows, cols), f32),
            vmem((rows, cols), bf16),
            vmem((rows, LANES), f32),
            vmem((rows, LANES), f32),
            vmem((rows, LANES), f32),
            vmem((rows // 8, cols), f32),
            vmem((rows // 8, cols), f32),
            vmem((1, cols), f32),
            vmem((ITERS + 1, nc, 2, rows), f32),
            vmem((ITERS, nr, 2, cols), f32),
            vmem((hi, rows, kn), bf16),
            vmem((hi, rows, kn), bf16),
            vmem((hi, rows, kn), bf16),
            vmem((hi, rows, kn), bf16),
            vmem((hi, rows, kn), bf16),
            vmem((rows, kn), f32),
            vmem((rows, kn), bf16),
            vmem((rows, kn), bf16),
            vmem((rows, kn), bf16),
            vmem((2, 1, rows), f32),
            vmem((1, cols), f32),
            dma((2,)),
            dma((3, hi)), dma((nc,)),
            dma((4, nr, 2)), dma((nr, 2)),
            dma((ITERS + 1, nc)), dma((ITERS + 1, nc)),
            dma((ITERS, nr)), dma((ITERS, nr)),
            dma((hi, 4)), dma((hi, 4)), dma((hi, 4)), dma((hi, 4)), dma((hi, 4)), dma((hi, 4)),
            dma((3,)), dma((3,)), dma((4,)), dma((4,)),
        ],
        compiler_params=pltpu.CompilerParams(
            collective_id=0, has_side_effects=True, vmem_limit_bytes=58 * 2**20
        ),
        cost_estimate=pl.CostEstimate(
            flops=4 * rows * cols * kl * nr, bytes_accessed=8 * 2**20, transcendentals=7 * rows * cols
        ),
    )(noise, latents)
    return transported, row_potential.reshape(rows), col_potential.reshape(cols)


def solution(mesh):
    in_specs = (P("row", "col"), P("col", "row"))
    out_specs = (P("row", "col"), P("row"), P("col"))
    return jax.shard_map(
        functools.partial(on_device, mesh.shape["row"], mesh.shape["col"]),
        mesh=mesh, in_specs=in_specs, out_specs=out_specs, check_vma=False,
    )
```
